32 devices in a mesh: groups: 2 (over x), bus: 16 (over z, y, core).
Axes of the slice: x: 2, y: 2, z: 4, core: 2. Of those that a mesh axis runs over, the one named last changes fastest.
Arguments:
- generation: float32 [512, 32], P('bus', 'groups'), parts along dimension 1, may hold values from 0 to 1
- charging: float32 [32, 512], P('groups', 'bus'), parts along dimension 0, may hold values from -1.5 to 1.5
- flow_dual: float32 [4096, 32], P('bus', 'groups'), parts along dimension 1, may hold values from -3 to 3
- energy_dual: float32 [32, 512], P('groups', 'bus'), parts along dimension 0, may hold values from -1.6 to 1.6
- shift_factors: float32 [4096, 16384], P(None, 'bus'), may hold values from -0.0625 to 0.0625
- load_units: int32 [16384, 32], P('bus', 'groups'), parts along dimension 1, may hold values from 0 to 59
- generator_bus: int32 [512], P('bus'), may hold values from 0 to 16383, as said below
- storage_bus: int32 [512], P('bus'), may hold values from 0 to 16383, as said below
- generator_cost: float32 [512], P('bus'), may hold values from 0.05 to 0.5
- generator_max: float32 [512], P('bus'), may hold values from 1 to 4
- charging_max: float32 [512], replicated, may hold values from 2 to 4
- energy_init: float32 [512], replicated, may hold values from 0.5 to 2
- energy_max: float32 [512], replicated, may hold values from 2.5 to 4
- line_max: float32 [4096], P('bus'), may hold values from 0.5 to 3
Outputs:
- generation_new: float32 [512, 32], P('bus', 'groups'), parts along dimension 1
- charging_new: float32 [32, 512], P('groups', 'bus'), parts along dimension 0
- flow_dual_new: float32 [4096, 32], P('bus', 'groups'), parts along dimension 1
- energy_dual_new: float32 [32, 512], P('groups', 'bus'), parts along dimension 0
The draws below stay inside these ranges and needn't reach their ends.
There are 2 independent parts, one for each index of `groups`. The reference program is written for one: setup_inputs(seed, part) draws one part's arguments, and reference() takes and returns one part's arrays. A program takes and returns all parts, laid end to end along the dimension named above; an argument that names none is the same for every part. Nothing has to cross between parts.
Inputs may be any that keep to these rules, and one draw needn't show every extreme that they name: `generator_bus`: generator g sits at one of the buses g // 32 * 1024 to (g // 32 + 1) * 1024 - 1. `storage_bus`: storage unit k sits at one of the buses k // 32 * 1024 to (k // 32 + 1) * 1024 - 1.
All inputs are finite; a program needn't handle non-finite values.
Results may differ from the reference program's by a relative error of at most 0.00023.
Values sent between devices are 32-bit elements; how exact they have to be, the bound alone decides.
A program may use at most 64 MiB of HBM per device.

```python
import math
import jax
import jax.numpy as jnp
from jax import lax

B = 16384
L = 4096
GEN_DEV = 32
STOR_DEV = 32
ITERS = 3
H = 16
NG = 512
NS = 512
N_BUS = 16


def draw_generator_bus(key, part):
    block = B // N_BUS
    owner = jnp.arange(NG, dtype=jnp.int32) // GEN_DEV
    offset = jax.random.randint(jax.random.fold_in(key, 11), (NG,), 0, block, dtype=jnp.int32)
    return owner * block + offset


def draw_storage_bus(key, part):
    block = B // N_BUS
    owner = jnp.arange(NS, dtype=jnp.int32) // STOR_DEV
    offset = jax.random.randint(jax.random.fold_in(key, 23), (NS,), 0, block, dtype=jnp.int32)
    return owner * block + offset


def touch_ends(values, rng, low, high):
    longest = values.shape.index(max(values.shape))
    spots = []
    for shift in (0, 1):
        where = [jax.random.randint(jax.random.fold_in(rng, axis), (), 0, length) for axis, length in enumerate(values.shape)]
        where[longest] = (where[longest] + shift) % values.shape[longest]
        spots.append(tuple(where))
    return values.at[spots[0]].set(low).at[spots[1]].set(high)


def spiked(drawn, rng, source, target, parts, factor):
    owner, partner = [(jnp.arange(drawn.shape[axis_at]) // (drawn.shape[axis_at] // parts)).reshape([-1 if axis == axis_at else 1 for axis in range(drawn.ndim)]) for axis_at in (source, target)]
    chosen = jax.random.permutation(rng, parts)[partner]
    strong = (owner == chosen) | (owner == (partner + parts // 2) % parts)
    return jnp.where(strong, factor * drawn, drawn)


def level_of(stream_key, extent, shards, least, largest):
    def one(position, parts):
        heights = jax.random.uniform(jax.random.fold_in(jax.random.fold_in(stream_key, 6), position), (parts,), jnp.float32, least / len(shards), largest / len(shards))
        return jnp.repeat(jnp.exp(heights), extent[position] // parts).reshape((-1,) + (1,) * (len(extent) - position - 1))

    loudness = one(*shards[0])
    for cut in shards[1:]:
        loudness = loudness * one(*cut)
    return loudness


def scatter_about(stream_key, dims, spread, reach, split=(), held_as=jnp.bfloat16):
    factor_of = level_of(stream_key, dims, split, -0.22, 0.18) if split else 1.0
    drawn = jax.random.normal(stream_key, dims, jnp.float32) * spread * factor_of
    return jnp.minimum(jnp.maximum(drawn, -reach), reach).astype(held_as)


def bell_draw_with(own_key, shape, width, limit, shards, heavy, held_as=jnp.bfloat16):
    result = width * jax.random.normal(own_key, shape, jnp.float32)
    if shards:
        result = result * level_of(own_key, shape, shards, -0.22, 0.18)
    return jnp.clip(spiked(result, jax.random.fold_in(own_key, 3), *heavy), -limit, limit).astype(held_as)


def setup_inputs(seed: int = 0, part: int = 0) -> dict:
    key_list = jax.random.split(jax.random.key(seed), 15)
    part_splits = jax.random.split(jax.random.fold_in(key_list[14], part), 15)
    generation = jnp.clip(1.0 * jax.random.uniform(part_splits[0], (NG, H), jnp.float32) ** level_of(part_splits[0], (NG, H), ((0, 16),), -0.2, 0.2), 0.0, 1.0)
    charging = jnp.clip(jax.random.uniform(part_splits[1], (H, NS), jnp.float32, -1.5, 1.5) * level_of(part_splits[1], (H, NS), ((1, 16),), -0.4, 0.0), -1.5, 1.5)
    flow_dual = scatter_about(part_splits[2], (L, H), 0.5, 3.0, ((0, 16),), jnp.float32)
    energy_dual = scatter_about(part_splits[3], (H, NS), 0.2, 1.6, ((1, 16),), jnp.float32)
    shift_factors = bell_draw_with(key_list[4], (L, B), B ** -0.5, 0.0625, ((1, 16),), (1, 0, 16, 2.0), jnp.float32)
    load_units = touch_ends(jax.random.randint(part_splits[5], (B, H), 0, 60), jax.random.fold_in(part_splits[5], 1), 0, 59).astype(jnp.int32)
    generator_bus = draw_generator_bus(jax.random.fold_in(key_list[14], 71), part)
    storage_bus = draw_storage_bus(jax.random.fold_in(key_list[14], 71), part)
    generator_cost = jnp.clip(jnp.exp(math.log(0.5) - 2.3025851 * jax.random.uniform(key_list[8], (NG,), jnp.float32) ** level_of(key_list[8], (NG,), ((0, 16),), -0.2, 0.2)), 0.05, 0.5)
    generator_max = jnp.clip(jnp.exp(math.log(4.0) - 1.3862944 * jax.random.uniform(key_list[9], (NG,), jnp.float32) ** level_of(key_list[9], (NG,), ((0, 16),), -0.2, 0.2)), 1.0, 4.0)
    charging_max = jnp.clip(jax.random.uniform(key_list[10], (NS,), jnp.float32, 2.0, 4.0), 2.0, 4.0)
    energy_init = jnp.clip(jax.random.uniform(key_list[11], (NS,), jnp.float32, 0.5, 2.0), 0.5, 2.0)
    energy_max = jnp.clip(jax.random.uniform(key_list[12], (NS,), jnp.float32, 2.5, 4.0), 2.5, 4.0)
    line_max = jnp.clip(0.5 + 2.5 * jax.random.uniform(key_list[13], (L,), jnp.float32) ** level_of(key_list[13], (L,), ((0, 16),), -0.2, 0.2), 0.5, 3.0)
    return {"generation": generation, "charging": charging, "flow_dual": flow_dual, "energy_dual": energy_dual, "shift_factors": shift_factors, "load_units": load_units, "generator_bus": generator_bus, "storage_bus": storage_bus, "generator_cost": generator_cost, "generator_max": generator_max, "charging_max": charging_max, "energy_init": energy_init, "energy_max": energy_max, "line_max": line_max}


primal_step = 0.5
dual_step = 0.5
energy_step = 0.05
efficiency = 0.95
interval = 0.125
load_unit = 0.05


def injection(gen_part, charge_part, load_units, generator_bus, storage_bus):
    from_generators = jax.ops.segment_sum(gen_part, generator_bus, num_segments=B)
    from_storage = jax.ops.segment_sum(charge_part.T, storage_bus, num_segments=B)
    return from_generators - from_storage - load_units.astype(jnp.float32) * load_unit


def reference(generation, charging, flow_dual, energy_dual, shift_factors, load_units, generator_bus, storage_bus, generator_cost, generator_max, charging_max, energy_init, energy_max, line_max):
    for iteration in range(ITERS):
        prices = jnp.dot(shift_factors.T, flow_dual, precision=lax.Precision.HIGHEST, preferred_element_type=jnp.float32)
        later_sum = jnp.flip(jnp.cumsum(jnp.flip(energy_dual, 0), axis=0), 0)
        gen_step = jnp.clip(generation - primal_step * (generator_cost[:, None] + prices[generator_bus]), 0.0, generator_max[:, None])
        gradient = efficiency * interval * later_sum - prices[storage_bus].T
        charge_step = jnp.clip(charging - primal_step * gradient, -charging_max[None, :], charging_max[None, :])
        gen_bar = 2.0 * gen_step - generation
        charge_bar = 2.0 * charge_step - charging
        injected = injection(gen_bar, charge_bar, load_units, generator_bus, storage_bus)
        line_flows = jnp.dot(shift_factors, injected, precision=lax.Precision.HIGHEST, preferred_element_type=jnp.float32)
        moved = flow_dual + dual_step * line_flows
        flow_dual = moved - dual_step * jnp.clip(moved / dual_step, -line_max[:, None], line_max[:, None])
        energy = energy_init[None, :] + efficiency * interval * jnp.cumsum(charge_bar, axis=0)
        shifted = energy_dual + energy_step * energy
        energy_dual = shifted - energy_step * jnp.clip(shifted / energy_step, 0.0, energy_max[None, :])
        generation = gen_step
        charging = charge_step
    return generation, charging, flow_dual, energy_dual
```

```python
import functools

import jax
import jax.numpy as jnp
from jax import lax
from jax.experimental import pallas as pl
from jax.experimental.pallas import tpu as pltpu
from jax.sharding import PartitionSpec as P

ITERS = 3
LANES = 128
MESH = pl.DeviceIdType.MESH

primal_step = 0.5
dual_step = 0.5
energy_step = 0.05
efficiency = 0.95
interval = 0.125
load_unit = 0.05
highest = lax.Precision.HIGHEST
across_first = (((0,), (0,)), ((), ()))
across_second = (((1,), (1,)), ((), ()))
inner_pair = (((1,), (0,)), ((), ()))


def contract(left, right, dims):
    return lax.dot_general(left, right, dims, precision=highest, preferred_element_type=jnp.float32)


def reverse_cumsum(values):
    return jnp.flip(jnp.cumsum(jnp.flip(values, 0), axis=0), 0)


def clip_dual(shifted, step_size, low_bound, high_bound):
    return shifted - step_size * jnp.clip(shifted / step_size, low_bound, high_bound)


def split_bf16(values):
    high = values.astype(jnp.bfloat16)
    return high, (values - high.astype(jnp.float32)).astype(jnp.bfloat16)


def running_sum(values, backward):
    rows = values.shape[0]
    row = lax.broadcasted_iota(jnp.int32, values.shape, 0)
    step = 1
    while step < rows:
        if backward:
            moved = jnp.where(row < rows - step, pltpu.roll(values, rows - step, 0), 0.0)
        else:
            moved = jnp.where(row >= step, pltpu.roll(values, step, 0), 0.0)
        values = values + moved
        step *= 2
    return values


def iterate_kernel(
    n_bus,
    gen_ref,
    charge_ref,
    dual_ref,
    energy_ref,
    factors_ref,
    load_ref,
    gen_bus_ref,
    stor_bus_ref,
    cost_ref,
    gen_max_ref,
    charge_max_ref,
    init_ref,
    energy_max_ref,
    line_max_ref,
    gen_out,
    charge_out,
    dual_out,
    energy_out,
    factors_buf,
    place_buf,
    pack_own,
    pack_sib,
    cols_send,
    cols_recv,
    weight_buf,
    demand_buf,
    dual_buf,
    flow_send,
    flow_recv,
    price_send,
    price_recv,
    factors_sem,
    pack_sem,
    cols_sems,
    dual_send_sem,
    dual_recv_sem,
    flow_send_sem,
    flow_recv_sem,
    price_sem,
):
    chips = n_bus // 2
    hours, units = gen_ref.shape
    block = dual_ref.shape[1]
    buses = factors_ref.shape[1]
    half = 2 * units
    width = 2 * half
    me = lax.axis_index("bus")
    core = lax.rem(me, 2)
    chip = lax.div(me, 2)
    sibling = me + 1 - 2 * core

    def peer(k):
        return lax.rem(chip + k, chips)

    def load_factors(i, parity):
        b = 2 * i + parity
        start = pl.multiple_of(b * block, block)
        return pltpu.make_async_copy(
            factors_ref.at[pl.ds(start, block), :], factors_buf.at[b], factors_sem.at[b]
        )

    @pl.loop(0, chips)
    def _(i):
        load_factors(i, 1 - core).start()

    @pl.loop(0, chips)
    def _(i):
        load_factors(i, core).start()

    barrier = pltpu.get_barrier_semaphore()
    for k in range(1, chips):
        pl.semaphore_signal(
            barrier, inc=1, device_id={"bus": 2 * peer(k) + core}, device_id_type=MESH
        )
    pl.semaphore_signal(barrier, inc=1, device_id={"bus": sibling}, device_id_type=MESH)
    pl.semaphore_wait(barrier, chips)

    def send_dual(t, k):
        source = dual_ref if t == 0 else dual_buf.at[t, chip]
        return pltpu.make_async_remote_copy(
            src_ref=source,
            dst_ref=dual_buf.at[t, chip],
            send_sem=dual_send_sem.at[t, k],
            recv_sem=dual_recv_sem.at[t, chip],
            device_id={"bus": 2 * peer(k) + core},
            device_id_type=MESH,
        )

    def recv_dual(t, c):
        return pltpu.make_async_remote_copy(
            src_ref=dual_buf.at[t, c],
            dst_ref=dual_buf.at[t, c],
            send_sem=dual_send_sem.at[t, 0],
            recv_sem=dual_recv_sem.at[t, c],
            device_id={"bus": sibling},
            device_id_type=MESH,
        )

    def send_flow(t, k):
        return pltpu.make_async_remote_copy(
            src_ref=flow_send.at[t, k],
            dst_ref=flow_recv.at[t, chip],
            send_sem=flow_send_sem.at[t, k],
            recv_sem=flow_recv_sem.at[t, chip],
            device_id={"bus": 2 * peer(k) + core},
            device_id_type=MESH,
        )

    def recv_flow(t, c):
        return pltpu.make_async_remote_copy(
            src_ref=flow_recv.at[t, c],
            dst_ref=flow_recv.at[t, c],
            send_sem=flow_send_sem.at[t, 0],
            recv_sem=flow_recv_sem.at[t, c],
            device_id={"bus": sibling},
            device_id_type=MESH,
        )

    def to_sibling(source, target, sems):
        return pltpu.make_async_remote_copy(
            src_ref=source,
            dst_ref=target,
            send_sem=sems.at[0],
            recv_sem=sems.at[1],
            device_id={"bus": sibling},
            device_id_type=MESH,
        )

    for k in range(1, chips):
        send_dual(0, k).start()

    gens = slice(0, units)
    stors = slice(units, half)
    pack_own[...] = jnp.zeros_like(pack_own)
    pack_own[0, :, gens] = gen_ref[...]
    pack_own[0, :, stors] = charge_ref[...]
    pack_own[1, :, stors] = energy_ref[...]
    pack_own[2, 0:1, gens] = cost_ref[...]
    pack_own[2, 1:2, gens] = gen_max_ref[...]
    first = me * units
    lane_start = pl.multiple_of(lax.div(first, LANES) * LANES, LANES)
    shift = lax.rem(units - lax.rem(first, LANES) + LANES, LANES)
    for row, ref in ((1, charge_max_ref), (2, init_ref), (3, energy_max_ref)):
        chunk = jnp.broadcast_to(ref[0:1, pl.ds(lane_start, LANES)], (8, LANES))
        pack_own[2, row : row + 1, stors] = pltpu.roll(chunk, shift, 1)[0:1, stors]
    send_pack = to_sibling(pack_own, pack_sib, pack_sem)
    send_pack.start()

    pack_index = jnp.full((8, LANES), -1, jnp.int32)
    lane8 = lax.broadcasted_iota(jnp.int32, (8, LANES), 1)
    for at, ref in ((0, gen_bus_ref), (units, stor_bus_ref)):
        padded = jnp.concatenate([ref[...], jnp.zeros((1, LANES - units), jnp.int32)], axis=1)
        padded = pltpu.roll(jnp.broadcast_to(padded, (8, LANES)), at, 1)
        pack_index = jnp.where((lane8 >= at) & (lane8 < at + units), padded - me * buses, pack_index)
    bus_id = lax.broadcasted_iota(jnp.int32, (buses, LANES), 0)
    onehot = jnp.where(bus_id == pack_index[0:1, :], 1.0, 0.0)
    loads = jnp.concatenate(
        [
            jnp.zeros((half, buses), jnp.float32),
            load_ref[...].astype(jnp.float32),
            jnp.zeros((LANES - half - hours, buses), jnp.float32),
        ],
        axis=0,
    )
    place_buf[...] = (onehot + loads.T).astype(jnp.bfloat16)

    def take_columns(b):
        high, low = split_bf16(factors_buf[b])
        place = place_buf[...]
        taken = jnp.dot(high, place, preferred_element_type=jnp.float32) + jnp.dot(
            low, place, preferred_element_type=jnp.float32
        )
        return taken.T[: half + hours]

    def swap_columns(i):
        return pltpu.make_async_remote_copy(
            src_ref=cols_send.at[i],
            dst_ref=cols_recv.at[i],
            send_sem=cols_sems.at[0, i],
            recv_sem=cols_sems.at[1, i],
            device_id={"bus": sibling},
            device_id_type=MESH,
        )

    @pl.loop(0, chips)
    def _(i):
        load_factors(i, 1 - core).wait()
        cols_send[i] = take_columns(2 * i + 1 - core)
        swap_columns(i).start()

    @pl.loop(0, chips)
    def _(i):
        load_factors(i, core).wait()
        mine = take_columns(2 * i + core)
        swap_columns(i).wait()
        other = cols_recv[i]
        high, low = split_bf16(jnp.concatenate([mine[:half], other[:half]], axis=0))
        weight_buf[i, 0:width] = high
        weight_buf[i, width : 2 * width] = low
        demand_buf[i] = load_unit * (mine[half:] + other[half:])

    send_pack.wait()
    state = pack_own[0] + pltpu.roll(pack_sib[0], half, 1)
    energy_dual = pack_own[1] + pltpu.roll(pack_sib[1], half, 1)
    params = pack_own[2] + pltpu.roll(pack_sib[2], half, 1)
    cost, upper, start_energy, energy_limit = (params[r : r + 1] for r in range(4))
    lane = lax.broadcasted_iota(jnp.int32, (hours, width), 1)
    is_gen = lax.rem(lane, half) < units
    lower = jnp.where(is_gen, 0.0, -upper)
    later = running_sum(energy_dual, True)
    own_dual = dual_ref[...]
    line_max = line_max_ref[...]

    for t in range(ITERS):
        total = jnp.zeros((2 * hours, 2 * width), jnp.float32)
        for k in range(chips):
            c = peer(chips - k)
            if k == 0:
                dual = own_dual
            else:
                recv_dual(t, c).wait_recv()
                dual = dual_buf[t, c]
            pieces = jnp.concatenate(split_bf16(dual), axis=0)
            total = total + lax.dot_general(
                pieces, weight_buf[c], across_second, preferred_element_type=jnp.float32
            )
        total = total[:hours] + total[hours:]
        part = total[:, :width] + total[:, width:]
        price_send[t] = part
        swap_prices = to_sibling(price_send.at[t], price_recv.at[t], price_sem.at[t])
        swap_prices.start()
        swap_prices.wait()
        prices = part + pltpu.roll(price_recv[t], half, 1)

        gradient = jnp.where(is_gen, cost + prices, efficiency * interval * later - prices)
        step = jnp.clip(state - primal_step * gradient, lower, upper)
        bar = 2.0 * step - state
        state = step
        high, low = split_bf16(jnp.where(is_gen, bar, -bar))
        pieces = jnp.concatenate(
            [jnp.concatenate([high, high], axis=1), jnp.concatenate([low, low], axis=1)], axis=0
        )

        def flows(c):
            out = jnp.dot(pieces, weight_buf[c], preferred_element_type=jnp.float32)
            return out[:hours] + out[hours:] - demand_buf[c]

        for k in range(1, chips):
            flow_send[t, k] = flows(peer(k))
            send_flow(t, k).start()
        line_flows = flows(chip)
        energy = start_energy + efficiency * interval * running_sum(bar, False)
        energy_dual = clip_dual(energy_dual + energy_step * energy, energy_step, 0.0, energy_limit)
        if t + 1 < ITERS:
            later = running_sum(energy_dual, True)
        for k in range(1, chips):
            c = peer(chips - k)
            recv_flow(t, c).wait_recv()
            line_flows = line_flows + flow_recv[t, c]
        own_dual = clip_dual(own_dual + dual_step * line_flows, dual_step, -line_max, line_max)
        if t + 1 < ITERS:
            dual_buf[t + 1, chip] = own_dual
            for k in range(1, chips):
                send_dual(t + 1, k).start()

    dual_out[...] = own_dual
    gen_out[...] = state[:, gens]
    charge_out[...] = state[:, stors]
    energy_out[...] = energy_dual[:, stors]
    for t in range(ITERS):
        for k in range(1, chips):
            send_dual(t, k).wait_send()
            send_flow(t, k).wait_send()


def on_device_kernel(
    generation,
    charging,
    flow_dual,
    energy_dual,
    shift_factors,
    load_units,
    generator_bus,
    storage_bus,
    generator_cost,
    generator_max,
    charging_max,
    energy_init,
    energy_max,
    line_max,
):
    lines, buses = shift_factors.shape
    units, hours = generation.shape
    block = flow_dual.shape[0]
    n_bus = lines // block
    chips = n_bus // 2
    half = 2 * units
    width = 2 * half
    vmem = pl.BlockSpec(memory_space=pltpu.VMEM)
    in_specs = [vmem] * 14
    in_specs[4] = pl.BlockSpec(memory_space=pltpu.HBM)
    f32 = jnp.float32
    dma = pltpu.SemaphoreType.DMA
    gen_new, charge_new, dual_new, energy_new = pl.pallas_call(
        functools.partial(iterate_kernel, n_bus),
        out_shape=(
            jax.ShapeDtypeStruct((hours, units), f32),
            jax.ShapeDtypeStruct((hours, units), f32),
            jax.ShapeDtypeStruct((hours, block), f32),
            jax.ShapeDtypeStruct((hours, units), f32),
        ),
        in_specs=in_specs,
        out_specs=(vmem,) * 4,
        scratch_shapes=[
            pltpu.VMEM((n_bus, block, buses), f32),
            pltpu.VMEM((buses, LANES), jnp.bfloat16),
            pltpu.VMEM((3, hours, width), f32),
            pltpu.VMEM((3, hours, width), f32),
            pltpu.VMEM((chips, half + hours, block), f32),
            pltpu.VMEM((chips, half + hours, block), f32),
            pltpu.VMEM((chips, 2 * width, block), jnp.bfloat16),
            pltpu.VMEM((chips, hours, block), f32),
            pltpu.VMEM((ITERS, chips, hours, block), f32),
            pltpu.VMEM((ITERS, chips, hours, block), f32),
            pltpu.VMEM((ITERS, chips, hours, block), f32),
            pltpu.VMEM((ITERS, hours, width), f32),
            pltpu.VMEM((ITERS, hours, width), f32),
            dma((n_bus,)),
            dma((2,)),
            dma((2, chips)),
            dma((ITERS, chips)),
            dma((ITERS, chips)),
            dma((ITERS, chips)),
            dma((ITERS, chips)),
            dma((ITERS, 2)),
        ],
        compiler_params=pltpu.CompilerParams(
            collective_id=0, has_side_effects=True, vmem_limit_bytes=52 * 1024 * 1024
        ),
    )(
        generation.T,
        charging,
        flow_dual.T,
        energy_dual,
        shift_factors,
        load_units.T,
        generator_bus[None, :],
        storage_bus[None, :],
        generator_cost[None, :],
        generator_max[None, :],
        charging_max[None, :],
        energy_init[None, :],
        energy_max[None, :],
        line_max[None, :],
    )
    return gen_new.T, charge_new, dual_new.T, energy_new


def on_device(
    generation,
    charging,
    flow_dual,
    energy_dual,
    shift_factors,
    load_units,
    generator_bus,
    storage_bus,
    generator_cost,
    generator_max,
    charging_max,
    energy_init,
    energy_max,
    line_max,
):
    bus_local = shift_factors.shape[1]
    gen_local = generator_bus.shape[0]
    stor_local = storage_bus.shape[0]
    own_index = lax.axis_index("bus")
    bus_ids = lax.broadcasted_iota(jnp.int32, (bus_local, 1), 0) + own_index * bus_local
    gen_onehot = (generator_bus[None, :] == bus_ids).astype(jnp.float32)
    stor_onehot = (storage_bus[None, :] == bus_ids).astype(jnp.float32)
    columns = contract(shift_factors, jnp.concatenate([gen_onehot, stor_onehot], axis=1), inner_pair)
    demand = load_units.astype(jnp.float32) * load_unit
    demand_flows = contract(shift_factors, demand, inner_pair)
    unit_cost = generator_cost[:, None]
    ceiling = generator_max[:, None]
    first_slot = own_index * stor_local
    charge_limit = lax.dynamic_slice_in_dim(charging_max, first_slot, stor_local)[None, :]
    start_energy = lax.dynamic_slice_in_dim(energy_init, first_slot, stor_local)[None, :]
    energy_limit = lax.dynamic_slice_in_dim(energy_max, first_slot, stor_local)[None, :]
    for iteration in range(ITERS):
        prices = contract(columns, lax.all_gather(flow_dual, "bus", axis=0, tiled=True), across_first)
        gen_step = jnp.clip(
            generation - primal_step * (unit_cost + prices[:gen_local]), 0.0, ceiling
        )
        gen_bar = 2.0 * gen_step - generation
        stor_prices = prices[gen_local:].T
        gradient = efficiency * interval * reverse_cumsum(energy_dual) - stor_prices
        charge_step = jnp.clip(charging - primal_step * gradient, -charge_limit, charge_limit)
        bar_bus = 2.0 * charge_step - charging
        energy = start_energy + efficiency * interval * jnp.cumsum(bar_bus, axis=0)
        energy_dual = clip_dual(energy_dual + energy_step * energy, energy_step, 0.0, energy_limit)
        charging = charge_step
        bars = jnp.concatenate([gen_bar, -bar_bus.T], axis=0)
        line_flows = lax.psum_scatter(
            contract(columns, bars, inner_pair) - demand_flows, "bus", scatter_dimension=0, tiled=True
        )
        flow_dual = clip_dual(
            flow_dual + dual_step * line_flows, dual_step, -line_max[:, None], line_max[:, None]
        )
        generation = gen_step
    return (generation, charging, flow_dual, energy_dual)


def fits_kernel(n_bus, generation, charging, flow_dual, shift_factors, storage_bus):
    units = generation.shape[0] // n_bus
    stors = storage_bus.shape[0] // n_bus
    block = flow_dual.shape[0] // n_bus
    hours = charging.shape[0] // 2
    buses = shift_factors.shape[1] // n_bus
    return (
        n_bus % 2 == 0
        and units == stors
        and 4 * units == LANES
        and hours == 16
        and block % LANES == 0
        and buses % LANES == 0
        and shift_factors.shape[0] * buses * 4 <= 2**24
    )


def solution(mesh):
    placed = (
        P("bus", "groups"),
        P("groups", "bus"),
        P("bus", "groups"),
        P("groups", "bus"),
        P(None, "bus"),
        P("bus", "groups"),
        P("bus"),
        P("bus"),
        P("bus"),
        P("bus"),
        P(),
        P(),
        P(),
        P("bus"),
    )
    n_bus = mesh.shape["bus"]

    def whole(*arrays):
        fits = mesh.shape["groups"] == 2 and fits_kernel(
            n_bus, arrays[0], arrays[1], arrays[2], arrays[4], arrays[7]
        )
        return jax.shard_map(
            on_device_kernel if fits else on_device,
            mesh=mesh,
            in_specs=placed,
            out_specs=(P("bus", "groups"), P("groups", "bus"), P("bus", "groups"), P("groups", "bus")),
            check_vma=False,
        )(*arrays)

    return whole
```

```python
import functools

import jax
import jax.numpy as jnp
from jax import lax
from jax.experimental import pallas as pl
from jax.experimental.pallas import tpu as pltpu
from jax.sharding import PartitionSpec as P

ITERS = 3
LANES = 128
VMEM_BYTES = 65472 * 1024
MESH = pl.DeviceIdType.MESH

primal_step = 0.5
dual_step = 0.5
energy_step = 0.05
efficiency = 0.95
interval = 0.125
load_unit = 0.05
highest = lax.Precision.HIGHEST
across_first = (((0,), (0,)), ((), ()))
across_second = (((1,), (1,)), ((), ()))
inner_pair = (((1,), (0,)), ((), ()))


def contract(left, right, dims):
    return lax.dot_general(left, right, dims, precision=highest, preferred_element_type=jnp.float32)


def reverse_cumsum(values):
    return jnp.flip(jnp.cumsum(jnp.flip(values, 0), axis=0), 0)


def clip_dual(shifted, step_size, low_bound, high_bound):
    return shifted - step_size * jnp.clip(shifted / step_size, low_bound, high_bound)


def split_bf16(values):
    high = values.astype(jnp.bfloat16)
    return high, (values - high.astype(jnp.float32)).astype(jnp.bfloat16)


def running_sum(values, backward):
    rows = values.shape[0]
    row = lax.broadcasted_iota(jnp.int32, values.shape, 0)
    step = 1
    while step < rows:
        if backward:
            moved = jnp.where(row < rows - step, pltpu.roll(values, rows - step, 0), 0.0)
        else:
            moved = jnp.where(row >= step, pltpu.roll(values, step, 0), 0.0)
        values = values + moved
        step *= 2
    return values


def iterate_kernel(
    n_bus,
    gen_hbm,
    charge_hbm,
    dual_hbm,
    energy_hbm,
    factors_hbm,
    load_hbm,
    gen_bus_hbm,
    stor_bus_hbm,
    cost_hbm,
    gen_max_hbm,
    charge_max_hbm,
    init_hbm,
    energy_max_hbm,
    line_max_hbm,
    gen_hbm_out,
    charge_hbm_out,
    dual_hbm_out,
    energy_hbm_out,
    gen_ref,
    charge_ref,
    energy_ref,
    load_ref,
    gen_bus_ref,
    stor_bus_ref,
    cost_ref,
    gen_max_ref,
    charge_max_ref,
    init_ref,
    energy_max_ref,
    line_max_ref,
    gen_out,
    charge_out,
    dual_out,
    energy_out,
    factors_buf,
    place_buf,
    pack_own,
    pack_sib,
    cols_send,
    cols_recv,
    weight_buf,
    turned_buf,
    demand_buf,
    dual_buf,
    flow_send,
    flow_recv,
    price_send,
    price_recv,
    input_sem,
    output_sem,
    factors_sem,
    pack_sem,
    cols_sems,
    dual_send_sem,
    dual_recv_sem,
    flow_send_sem,
    flow_recv_sem,
    price_sem,
):
    chips = n_bus // 2
    hours, units = gen_ref.shape
    block = dual_hbm.shape[1]
    buses = factors_hbm.shape[1]
    half = 2 * units
    width = 2 * half
    me = lax.axis_index("bus")
    core = lax.rem(me, 2)
    chip = lax.div(me, 2)
    sibling = me + 1 - 2 * core
    far_first = sorted(range(1, chips), key=lambda k: abs(2 * k - chips))

    def peer(k):
        return lax.rem(chip + k, chips)

    dual_in = pltpu.make_async_copy(dual_hbm, dual_buf.at[0, chip], input_sem.at[0])
    fetches = [
        pltpu.make_async_copy(source, target, input_sem.at[1 + at])
        for at, (source, target) in enumerate(
            (
                (load_hbm, load_ref),
                (gen_bus_hbm, gen_bus_ref),
                (stor_bus_hbm, stor_bus_ref),
                (gen_hbm, gen_ref),
                (charge_hbm, charge_ref),
                (energy_hbm, energy_ref),
                (cost_hbm, cost_ref),
                (gen_max_hbm, gen_max_ref),
                (charge_max_hbm, charge_max_ref),
                (init_hbm, init_ref),
                (energy_max_hbm, energy_max_ref),
                (line_max_hbm, line_max_ref),
            )
        )
    ]
    stores = [
        pltpu.make_async_copy(source, target, output_sem.at[at])
        for at, (source, target) in enumerate(
            (
                (gen_out, gen_hbm_out),
                (charge_out, charge_hbm_out),
                (energy_out, energy_hbm_out),
                (dual_out, dual_hbm_out),
            )
        )
    ]
    dual_in.start()
    for fetch in fetches:
        fetch.start()

    def load_factors(i, parity):
        b = 2 * i + parity
        start = pl.multiple_of(b * block, block)
        return pltpu.make_async_copy(
            factors_hbm.at[pl.ds(start, block), :], factors_buf.at[b], factors_sem.at[b]
        )

    @pl.loop(0, chips)
    def _(i):
        load_factors(i, 1 - core).start()

    @pl.loop(0, chips)
    def _(i):
        load_factors(i, core).start()

    barrier = pltpu.get_barrier_semaphore()
    for k in range(1, chips):
        pl.semaphore_signal(
            barrier, inc=1, device_id={"bus": 2 * peer(k) + core}, device_id_type=MESH
        )
    pl.semaphore_signal(barrier, inc=1, device_id={"bus": sibling}, device_id_type=MESH)

    def send_dual(t, k):
        return pltpu.make_async_remote_copy(
            src_ref=dual_buf.at[t, chip],
            dst_ref=dual_buf.at[t, chip],
            send_sem=dual_send_sem.at[t, k],
            recv_sem=dual_recv_sem.at[t, chip],
            device_id={"bus": 2 * peer(k) + core},
            device_id_type=MESH,
        )

    def recv_dual(t, c):
        return pltpu.make_async_remote_copy(
            src_ref=dual_buf.at[t, c],
            dst_ref=dual_buf.at[t, c],
            send_sem=dual_send_sem.at[t, 0],
            recv_sem=dual_recv_sem.at[t, c],
            device_id={"bus": sibling},
            device_id_type=MESH,
        )

    def send_flow(t, k):
        return pltpu.make_async_remote_copy(
            src_ref=flow_send.at[t, k],
            dst_ref=flow_recv.at[t, chip],
            send_sem=flow_send_sem.at[t, k],
            recv_sem=flow_recv_sem.at[t, chip],
            device_id={"bus": 2 * peer(k) + core},
            device_id_type=MESH,
        )

    def recv_flow(t, c):
        return pltpu.make_async_remote_copy(
            src_ref=flow_recv.at[t, c],
            dst_ref=flow_recv.at[t, c],
            send_sem=flow_send_sem.at[t, 0],
            recv_sem=flow_recv_sem.at[t, c],
            device_id={"bus": sibling},
            device_id_type=MESH,
        )

    def to_sibling(source, target, sems):
        return pltpu.make_async_remote_copy(
            src_ref=source,
            dst_ref=target,
            send_sem=sems.at[0],
            recv_sem=sems.at[1],
            device_id={"bus": sibling},
            device_id_type=MESH,
        )

    for fetch in fetches[:3]:
        fetch.wait()
    pack_index = jnp.full((8, LANES), -1, jnp.int32)
    lane8 = lax.broadcasted_iota(jnp.int32, (8, LANES), 1)
    for at, ref in ((0, gen_bus_ref), (units, stor_bus_ref)):
        padded = jnp.concatenate([ref[...], jnp.zeros((1, LANES - units), jnp.int32)], axis=1)
        padded = pltpu.roll(jnp.broadcast_to(padded, (8, LANES)), at, 1)
        pack_index = jnp.where((lane8 >= at) & (lane8 < at + units), padded - me * buses, pack_index)
    bus_id = lax.broadcasted_iota(jnp.int32, (buses, LANES), 0)
    onehot = jnp.where(bus_id == pack_index[0:1, :], 1.0, 0.0)
    loads = jnp.concatenate(
        [
            jnp.zeros((half, buses), jnp.float32),
            load_ref[...].astype(jnp.float32),
            jnp.zeros((LANES - half - hours, buses), jnp.float32),
        ],
        axis=0,
    )
    place = onehot + loads.T
    place_buf[0] = place.astype(jnp.bfloat16)
    place_buf[1] = pltpu.roll(place, half, 1).astype(jnp.bfloat16)

    for fetch in fetches[3:]:
        fetch.wait()
    gens = slice(0, units)
    stors = slice(units, half)
    pack_own[...] = jnp.zeros_like(pack_own)
    pack_own[0, :, gens] = gen_ref[...]
    pack_own[0, :, stors] = charge_ref[...]
    pack_own[1, :, stors] = energy_ref[...]
    pack_own[2, 0:1, gens] = cost_ref[...]
    pack_own[2, 1:2, gens] = gen_max_ref[...]
    first = me * units
    lane_start = pl.multiple_of(lax.div(first, LANES) * LANES, LANES)
    shift = lax.rem(units - lax.rem(first, LANES) + LANES, LANES)
    for row, ref in ((1, charge_max_ref), (2, init_ref), (3, energy_max_ref)):
        chunk = jnp.broadcast_to(ref[0:1, pl.ds(lane_start, LANES)], (8, LANES))
        pack_own[2, row : row + 1, stors] = pltpu.roll(chunk, shift, 1)[0:1, stors]

    pl.semaphore_wait(barrier, chips)
    dual_in.wait()
    for k in far_first:
        send_dual(0, k).start()
    send_pack = to_sibling(pack_own, pack_sib, pack_sem)
    send_pack.start()

    def take_columns(b, placed):
        high, low = split_bf16(factors_buf[b])
        place = place_buf[placed]
        return jnp.dot(high, place, preferred_element_type=jnp.float32) + jnp.dot(
            low, place, preferred_element_type=jnp.float32
        )

    def swap_columns(i):
        return pltpu.make_async_remote_copy(
            src_ref=cols_send.at[i],
            dst_ref=cols_recv.at[i],
            send_sem=cols_sems.at[0, i],
            recv_sem=cols_sems.at[1, i],
            device_id={"bus": sibling},
            device_id_type=MESH,
        )

    together = 2 if chips % 2 == 0 else 1

    @pl.loop(0, chips // together)
    def _(step):
        turns = [step * together + j for j in range(together)]
        for i in turns:
            load_factors(i, 1 - core).wait()
        for i in turns:
            cols_send[i] = take_columns(2 * i + 1 - core, 1)
        for i in turns:
            swap_columns(i).start()

    for k in reversed(far_first):
        recv_dual(0, peer(chips - k)).wait_recv()

    def collect(step, total):
        turns = [step * together + j for j in range(together)]
        for i in turns:
            load_factors(i, core).wait()
        for i in turns:
            swap_columns(i).wait()
        for i in turns:
            mine = take_columns(2 * i + core, 0)
            other = cols_recv[i]
            lane_at = lax.broadcasted_iota(jnp.int32, mine.shape, 1)
            columns = jnp.where(lane_at < half, mine, other)
            turned = jnp.concatenate(split_bf16(columns), axis=1)
            turned_buf[i] = turned
            high, low = split_bf16(columns.T)
            weight_buf[i, 0:width] = high
            weight_buf[i, width : 2 * width] = low
            demand = mine + pltpu.roll(other, half, 1)
            demand_buf[i] = load_unit * demand.T[half : half + hours]
            pieces = jnp.concatenate(split_bf16(dual_buf[0, i]), axis=0)
            total = total + jnp.dot(pieces, turned, preferred_element_type=jnp.float32)
        return total

    total = lax.fori_loop(
        0, chips // together, collect, jnp.zeros((2 * hours, 2 * width), jnp.float32)
    )

    send_pack.wait()
    state = pack_own[0] + pltpu.roll(pack_sib[0], half, 1)
    energy_dual = pack_own[1] + pltpu.roll(pack_sib[1], half, 1)
    params = pack_own[2] + pltpu.roll(pack_sib[2], half, 1)
    cost, upper, start_energy, energy_limit = (params[r : r + 1] for r in range(4))
    lane = lax.broadcasted_iota(jnp.int32, (hours, width), 1)
    is_gen = lax.rem(lane, half) < units
    lower = jnp.where(is_gen, 0.0, -upper)
    later = running_sum(energy_dual, True)
    own_dual = dual_buf[0, chip]
    line_max = line_max_ref[...]

    for t in range(ITERS):
        if t > 0:
            total = jnp.zeros((2 * hours, 2 * width), jnp.float32)
            for k in [0] + far_first[::-1]:
                c = peer(chips - k)
                if k == 0:
                    dual = own_dual
                else:
                    recv_dual(t, c).wait_recv()
                    dual = dual_buf[t, c]
                pieces = jnp.concatenate(split_bf16(dual), axis=0)
                total = total + jnp.dot(pieces, turned_buf[c], preferred_element_type=jnp.float32)
        total = total[:hours] + total[hours:]
        part = total[:, :width] + total[:, width:]
        price_send[t] = part
        swap_prices = to_sibling(price_send.at[t], price_recv.at[t], price_sem.at[t])
        swap_prices.start()
        swap_prices.wait()
        prices = part + pltpu.roll(price_recv[t], half, 1)

        gradient = jnp.where(is_gen, cost + prices, efficiency * interval * later - prices)
        step = jnp.clip(state - primal_step * gradient, lower, upper)
        bar = 2.0 * step - state
        state = step
        high, low = split_bf16(jnp.where(is_gen, bar, -bar))
        pieces = jnp.concatenate(
            [jnp.concatenate([high, high], axis=1), jnp.concatenate([low, low], axis=1)], axis=0
        )

        def flows(c):
            out = jnp.dot(pieces, weight_buf[c], preferred_element_type=jnp.float32)
            return out[:hours] + out[hours:] - demand_buf[c]

        for k in far_first:
            flow_send[t, k] = flows(peer(k))
            send_flow(t, k).start()
        line_flows = flows(chip)
        if t + 1 == ITERS:
            gen_out[...] = state[:, gens]
            charge_out[...] = state[:, stors]
            stores[0].start()
            stores[1].start()
        energy = start_energy + efficiency * interval * running_sum(bar, False)
        energy_dual = clip_dual(energy_dual + energy_step * energy, energy_step, 0.0, energy_limit)
        if t + 1 < ITERS:
            later = running_sum(energy_dual, True)
        else:
            energy_out[...] = energy_dual[:, stors]
            stores[2].start()
        for k in far_first[::-1]:
            c = peer(chips - k)
            recv_flow(t, c).wait_recv()
            line_flows = line_flows + flow_recv[t, c]
        own_dual = clip_dual(own_dual + dual_step * line_flows, dual_step, -line_max, line_max)
        if t + 1 < ITERS:
            dual_buf[t + 1, chip] = own_dual
            for k in far_first:
                send_dual(t + 1, k).start()

    dual_out[...] = own_dual
    stores[3].start()
    for t in range(ITERS):
        for k in range(1, chips):
            send_dual(t, k).wait_send()
            send_flow(t, k).wait_send()
    for store in stores:
        store.wait()


def store_kernel(*refs):
    count = len(refs) // 2
    sems = refs[-1]
    copies = [
        pltpu.make_async_copy(refs[at], refs[count + at], sems.at[at]) for at in range(count)
    ]
    for copy in copies:
        copy.start()
    for copy in copies:
        copy.wait()


def on_device_kernel(
    generation,
    charging,
    flow_dual,
    energy_dual,
    shift_factors,
    load_units,
    generator_bus,
    storage_bus,
    generator_cost,
    generator_max,
    charging_max,
    energy_init,
    energy_max,
    line_max,
):
    lines, buses = shift_factors.shape
    units, hours = generation.shape
    block = flow_dual.shape[0]
    n_bus = lines // block
    chips = n_bus // 2
    half = 2 * units
    width = 2 * half
    hbm = pl.BlockSpec(memory_space=pltpu.HBM)
    f32 = jnp.float32
    dma = pltpu.SemaphoreType.DMA
    arrays = (
        generation.T,
        charging,
        flow_dual.T,
        energy_dual,
        shift_factors,
        load_units.T,
        generator_bus[None, :],
        storage_bus[None, :],
        generator_cost[None, :],
        generator_max[None, :],
        charging_max[None, :],
        energy_init[None, :],
        energy_max[None, :],
        line_max[None, :],
    )
    out_shape = (
        jax.ShapeDtypeStruct((hours, units), f32),
        jax.ShapeDtypeStruct((hours, units), f32),
        jax.ShapeDtypeStruct((hours, block), f32),
        jax.ShapeDtypeStruct((hours, units), f32),
    )
    results = pl.pallas_call(
        functools.partial(iterate_kernel, n_bus),
        out_shape=out_shape,
        in_specs=[hbm] * len(arrays),
        out_specs=(hbm,) * 4,
        scratch_shapes=[
            pltpu.VMEM(array.shape, array.dtype)
            for at, array in enumerate(arrays)
            if at not in (2, 4)
        ]
        + [pltpu.VMEM(result.shape, f32) for result in out_shape]
        + [
            pltpu.VMEM((n_bus, block, buses), f32),
            pltpu.VMEM((2, buses, LANES), jnp.bfloat16),
            pltpu.VMEM((3, hours, width), f32),
            pltpu.VMEM((3, hours, width), f32),
            pltpu.VMEM((chips, block, LANES), f32),
            pltpu.VMEM((chips, block, LANES), f32),
            pltpu.VMEM((chips, 2 * width, block), jnp.bfloat16),
            pltpu.VMEM((chips, block, 2 * width), jnp.bfloat16),
            pltpu.VMEM((chips, hours, block), f32),
            pltpu.VMEM((ITERS, chips, hours, block), f32),
            pltpu.VMEM((ITERS, chips, hours, block), f32),
            pltpu.VMEM((ITERS, chips, hours, block), f32),
            pltpu.VMEM((ITERS, hours, width), f32),
            pltpu.VMEM((ITERS, hours, width), f32),
            dma((len(arrays) - 1,)),
            dma((4,)),
            dma((n_bus,)),
            dma((2,)),
            dma((2, chips)),
            dma((ITERS, chips)),
            dma((ITERS, chips)),
            dma((ITERS, chips)),
            dma((ITERS, chips)),
            dma((ITERS, 2)),
        ],
        compiler_params=pltpu.CompilerParams(
            collective_id=0, has_side_effects=True, vmem_limit_bytes=VMEM_BYTES
        ),
    )(*arrays)
    gen_new, charge_new, dual_new, energy_new = pl.pallas_call(
        store_kernel,
        out_shape=out_shape,
        in_specs=[hbm] * 4,
        out_specs=(hbm,) * 4,
        scratch_shapes=[dma((4,))],
        compiler_params=pltpu.CompilerParams(vmem_limit_bytes=VMEM_BYTES),
    )(*results)
    return gen_new.T, charge_new, dual_new.T, energy_new


def on_device(
    generation,
    charging,
    flow_dual,
    energy_dual,
    shift_factors,
    load_units,
    generator_bus,
    storage_bus,
    generator_cost,
    generator_max,
    charging_max,
    energy_init,
    energy_max,
    line_max,
):
    bus_local = shift_factors.shape[1]
    gen_local = generator_bus.shape[0]
    stor_local = storage_bus.shape[0]
    own_index = lax.axis_index("bus")
    bus_ids = lax.broadcasted_iota(jnp.int32, (bus_local, 1), 0) + own_index * bus_local
    gen_onehot = (generator_bus[None, :] == bus_ids).astype(jnp.float32)
    stor_onehot = (storage_bus[None, :] == bus_ids).astype(jnp.float32)
    columns = contract(shift_factors, jnp.concatenate([gen_onehot, stor_onehot], axis=1), inner_pair)
    demand = load_units.astype(jnp.float32) * load_unit
    demand_flows = contract(shift_factors, demand, inner_pair)
    unit_cost = generator_cost[:, None]
    ceiling = generator_max[:, None]
    first_slot = own_index * stor_local
    charge_limit = lax.dynamic_slice_in_dim(charging_max, first_slot, stor_local)[None, :]
    start_energy = lax.dynamic_slice_in_dim(energy_init, first_slot, stor_local)[None, :]
    energy_limit = lax.dynamic_slice_in_dim(energy_max, first_slot, stor_local)[None, :]
    for iteration in range(ITERS):
        prices = contract(columns, lax.all_gather(flow_dual, "bus", axis=0, tiled=True), across_first)
        gen_step = jnp.clip(
            generation - primal_step * (unit_cost + prices[:gen_local]), 0.0, ceiling
        )
        gen_bar = 2.0 * gen_step - generation
        stor_prices = prices[gen_local:].T
        gradient = efficiency * interval * reverse_cumsum(energy_dual) - stor_prices
        charge_step = jnp.clip(charging - primal_step * gradient, -charge_limit, charge_limit)
        bar_bus = 2.0 * charge_step - charging
        energy = start_energy + efficiency * interval * jnp.cumsum(bar_bus, axis=0)
        energy_dual = clip_dual(energy_dual + energy_step * energy, energy_step, 0.0, energy_limit)
        charging = charge_step
        bars = jnp.concatenate([gen_bar, -bar_bus.T], axis=0)
        line_flows = lax.psum_scatter(
            contract(columns, bars, inner_pair) - demand_flows, "bus", scatter_dimension=0, tiled=True
        )
        flow_dual = clip_dual(
            flow_dual + dual_step * line_flows, dual_step, -line_max[:, None], line_max[:, None]
        )
        generation = gen_step
    return (generation, charging, flow_dual, energy_dual)


def fits_kernel(n_bus, generation, charging, flow_dual, shift_factors, storage_bus):
    units = generation.shape[0] // n_bus
    stors = storage_bus.shape[0] // n_bus
    block = flow_dual.shape[0] // n_bus
    hours = charging.shape[0] // 2
    buses = shift_factors.shape[1] // n_bus
    return (
        n_bus % 2 == 0
        and units == stors
        and 4 * units == LANES
        and hours == 16
        and block % LANES == 0
        and buses % LANES == 0
        and shift_factors.shape[0] * buses * 4 <= 2**24
    )


def solution(mesh):
    placed = (
        P("bus", "groups"),
        P("groups", "bus"),
        P("bus", "groups"),
        P("groups", "bus"),
        P(None, "bus"),
        P("bus", "groups"),
        P("bus"),
        P("bus"),
        P("bus"),
        P("bus"),
        P(),
        P(),
        P(),
        P("bus"),
    )
    n_bus = mesh.shape["bus"]

    def whole(*arrays):
        fits = mesh.shape["groups"] == 2 and fits_kernel(
            n_bus, arrays[0], arrays[1], arrays[2], arrays[4], arrays[7]
        )
        return jax.shard_map(
            on_device_kernel if fits else on_device,
            mesh=mesh,
            in_specs=placed,
            out_specs=(P("bus", "groups"), P("groups", "bus"), P("bus", "groups"), P("groups", "bus")),
            check_vma=False,
        )(*arrays)

    return whole
```

```python
import functools

import jax
import jax.numpy as jnp
from jax import lax
from jax.experimental import pallas as pl
from jax.experimental.pallas import tpu as pltpu
from jax.sharding import PartitionSpec as P

ITERS = 3
LANES = 128
PARTS = 2
VMEM_BYTES = 65472 * 1024
MESH = pl.DeviceIdType.MESH

primal_step = 0.5
dual_step = 0.5
energy_step = 0.05
efficiency = 0.95
interval = 0.125
load_unit = 0.05
highest = lax.Precision.HIGHEST
across_first = (((0,), (0,)), ((), ()))
across_second = (((1,), (1,)), ((), ()))
inner_pair = (((1,), (0,)), ((), ()))


def contract(left, right, dims):
    return lax.dot_general(left, right, dims, precision=highest, preferred_element_type=jnp.float32)


def reverse_cumsum(values):
    return jnp.flip(jnp.cumsum(jnp.flip(values, 0), axis=0), 0)


def clip_dual(shifted, step_size, low_bound, high_bound):
    return shifted - step_size * jnp.clip(shifted / step_size, low_bound, high_bound)


def split_bf16(values):
    high = values.astype(jnp.bfloat16)
    return high, (values - high.astype(jnp.float32)).astype(jnp.bfloat16)


def running_sum(values, backward):
    rows = values.shape[0]
    row = lax.broadcasted_iota(jnp.int32, values.shape, 0)
    step = 1
    while step < rows:
        if backward:
            moved = jnp.where(row < rows - step, pltpu.roll(values, rows - step, 0), 0.0)
        else:
            moved = jnp.where(row >= step, pltpu.roll(values, step, 0), 0.0)
        values = values + moved
        step *= 2
    return values


def iterate_kernel(
    n_bus,
    gen_hbm,
    charge_hbm,
    dual_hbm,
    energy_hbm,
    factors_hbm,
    load_hbm,
    gen_bus_hbm,
    stor_bus_hbm,
    cost_hbm,
    gen_max_hbm,
    charge_max_hbm,
    init_hbm,
    energy_max_hbm,
    line_max_hbm,
    gen_hbm_out,
    charge_hbm_out,
    dual_hbm_out,
    energy_hbm_out,
    gen_ref,
    charge_ref,
    energy_ref,
    load_ref,
    gen_bus_ref,
    stor_bus_ref,
    cost_ref,
    gen_max_ref,
    charge_max_ref,
    init_ref,
    energy_max_ref,
    line_max_ref,
    gen_out,
    charge_out,
    dual_out,
    energy_out,
    factors_buf,
    place_buf,
    pack_own,
    pack_sib,
    cols_send,
    cols_recv,
    weight_buf,
    turned_buf,
    demand_buf,
    dual_buf,
    flow_send,
    flow_recv,
    price_send,
    price_recv,
    input_sem,
    output_sem,
    factors_sem,
    pack_sem,
    cols_sems,
    dual_send_sem,
    dual_recv_sem,
    flow_send_sem,
    flow_recv_sem,
    price_sem,
):
    chips = n_bus // 2
    hours, units = gen_ref.shape
    block = dual_hbm.shape[1]
    buses = factors_hbm.shape[1]
    half = 2 * units
    width = 2 * half
    me = lax.axis_index("bus")
    core = lax.rem(me, 2)
    chip = lax.div(me, 2)
    sibling = me + 1 - 2 * core
    far_first = sorted(range(1, chips), key=lambda k: abs(2 * k - chips))

    def peer(k):
        return lax.rem(chip + k, chips)

    dual_in = pltpu.make_async_copy(dual_hbm, dual_buf.at[0, chip], input_sem.at[0])
    fetches = [
        pltpu.make_async_copy(source, target, input_sem.at[1 + at])
        for at, (source, target) in enumerate(
            (
                (load_hbm, load_ref),
                (gen_bus_hbm, gen_bus_ref),
                (stor_bus_hbm, stor_bus_ref),
                (gen_hbm, gen_ref),
                (charge_hbm, charge_ref),
                (energy_hbm, energy_ref),
                (cost_hbm, cost_ref),
                (gen_max_hbm, gen_max_ref),
                (charge_max_hbm, charge_max_ref),
                (init_hbm, init_ref),
                (energy_max_hbm, energy_max_ref),
                (line_max_hbm, line_max_ref),
            )
        )
    ]
    stores = [
        pltpu.make_async_copy(source, target, output_sem.at[at])
        for at, (source, target) in enumerate(
            (
                (gen_out, gen_hbm_out),
                (charge_out, charge_hbm_out),
                (energy_out, energy_hbm_out),
                (dual_out, dual_hbm_out),
            )
        )
    ]
    dual_in.start()
    for fetch in fetches:
        fetch.start()

    def load_factors(i, parity):
        b = 2 * i + parity
        start = pl.multiple_of(b * block, block)
        return pltpu.make_async_copy(
            factors_hbm.at[pl.ds(start, block), :], factors_buf.at[b], factors_sem.at[b]
        )

    @pl.loop(0, chips)
    def _(i):
        load_factors(i, 1 - core).start()

    @pl.loop(0, chips)
    def _(i):
        load_factors(i, core).start()

    barrier = pltpu.get_barrier_semaphore()
    for k in range(1, chips):
        pl.semaphore_signal(
            barrier, inc=1, device_id={"bus": 2 * peer(k) + core}, device_id_type=MESH
        )
    pl.semaphore_signal(barrier, inc=1, device_id={"bus": sibling}, device_id_type=MESH)

    part_rows = hours // PARTS

    def rows(part):
        return slice(part * part_rows, (part + 1) * part_rows)

    def send_dual(t, k, part):
        return pltpu.make_async_remote_copy(
            src_ref=dual_buf.at[t, chip, rows(part)],
            dst_ref=dual_buf.at[t, chip, rows(part)],
            send_sem=dual_send_sem.at[t, part, k],
            recv_sem=dual_recv_sem.at[t, part, chip],
            device_id={"bus": 2 * peer(k) + core},
            device_id_type=MESH,
        )

    def recv_dual(t, c, part):
        return pltpu.make_async_remote_copy(
            src_ref=dual_buf.at[t, c, rows(part)],
            dst_ref=dual_buf.at[t, c, rows(part)],
            send_sem=dual_send_sem.at[t, part, 0],
            recv_sem=dual_recv_sem.at[t, part, c],
            device_id={"bus": sibling},
            device_id_type=MESH,
        )

    def send_flow(t, k, part):
        return pltpu.make_async_remote_copy(
            src_ref=flow_send.at[t, k, rows(part)],
            dst_ref=flow_recv.at[t, chip, rows(part)],
            send_sem=flow_send_sem.at[t, part, k],
            recv_sem=flow_recv_sem.at[t, part, chip],
            device_id={"bus": 2 * peer(k) + core},
            device_id_type=MESH,
        )

    def recv_flow(t, c, part):
        return pltpu.make_async_remote_copy(
            src_ref=flow_recv.at[t, c, rows(part)],
            dst_ref=flow_recv.at[t, c, rows(part)],
            send_sem=flow_send_sem.at[t, part, 0],
            recv_sem=flow_recv_sem.at[t, part, c],
            device_id={"bus": sibling},
            device_id_type=MESH,
        )

    def to_sibling(source, target, sems):
        return pltpu.make_async_remote_copy(
            src_ref=source,
            dst_ref=target,
            send_sem=sems.at[0],
            recv_sem=sems.at[1],
            device_id={"bus": sibling},
            device_id_type=MESH,
        )

    for fetch in fetches[:3]:
        fetch.wait()
    pack_index = jnp.full((8, LANES), -1, jnp.int32)
    lane8 = lax.broadcasted_iota(jnp.int32, (8, LANES), 1)
    for at, ref in ((0, gen_bus_ref), (units, stor_bus_ref)):
        padded = jnp.concatenate([ref[...], jnp.zeros((1, LANES - units), jnp.int32)], axis=1)
        padded = pltpu.roll(jnp.broadcast_to(padded, (8, LANES)), at, 1)
        pack_index = jnp.where((lane8 >= at) & (lane8 < at + units), padded - me * buses, pack_index)
    bus_id = lax.broadcasted_iota(jnp.int32, (buses, LANES), 0)
    onehot = jnp.where(bus_id == pack_index[0:1, :], 1.0, 0.0)
    loads = jnp.concatenate(
        [
            jnp.zeros((half, buses), jnp.float32),
            load_ref[...].astype(jnp.float32),
            jnp.zeros((LANES - half - hours, buses), jnp.float32),
        ],
        axis=0,
    )
    place = onehot + loads.T
    place_buf[0] = place.astype(jnp.bfloat16)
    place_buf[1] = pltpu.roll(place, half, 1).astype(jnp.bfloat16)

    for fetch in fetches[3:]:
        fetch.wait()
    gens = slice(0, units)
    stors = slice(units, half)
    pack_own[...] = jnp.zeros_like(pack_own)
    pack_own[0, :, gens] = gen_ref[...]
    pack_own[0, :, stors] = charge_ref[...]
    pack_own[1, :, stors] = energy_ref[...]
    pack_own[2, 0:1, gens] = cost_ref[...]
    pack_own[2, 1:2, gens] = gen_max_ref[...]
    first = me * units
    lane_start = pl.multiple_of(lax.div(first, LANES) * LANES, LANES)
    shift = lax.rem(units - lax.rem(first, LANES) + LANES, LANES)
    for row, ref in ((1, charge_max_ref), (2, init_ref), (3, energy_max_ref)):
        chunk = jnp.broadcast_to(ref[0:1, pl.ds(lane_start, LANES)], (8, LANES))
        pack_own[2, row : row + 1, stors] = pltpu.roll(chunk, shift, 1)[0:1, stors]

    pl.semaphore_wait(barrier, chips)
    dual_in.wait()
    for k in far_first:
        for part in range(PARTS):
            send_dual(0, k, part).start()
    send_pack = to_sibling(pack_own, pack_sib, pack_sem)
    send_pack.start()

    def take_columns(b, placed):
        high, low = split_bf16(factors_buf[b])
        place = place_buf[placed]
        return jnp.dot(high, place, preferred_element_type=jnp.float32) + jnp.dot(
            low, place, preferred_element_type=jnp.float32
        )

    def swap_columns(i):
        return pltpu.make_async_remote_copy(
            src_ref=cols_send.at[i],
            dst_ref=cols_recv.at[i],
            send_sem=cols_sems.at[0, i],
            recv_sem=cols_sems.at[1, i],
            device_id={"bus": sibling},
            device_id_type=MESH,
        )

    together = 2 if chips % 2 == 0 else 1

    @pl.loop(0, chips // together)
    def _(step):
        turns = [step * together + j for j in range(together)]
        for i in turns:
            load_factors(i, 1 - core).wait()
        for i in turns:
            cols_send[i] = take_columns(2 * i + 1 - core, 1)
        for i in turns:
            swap_columns(i).start()

    for k in reversed(far_first):
        for part in range(PARTS):
            recv_dual(0, peer(chips - k), part).wait_recv()

    def collect(step, total):
        turns = [step * together + j for j in range(together)]
        for i in turns:
            load_factors(i, core).wait()
        for i in turns:
            swap_columns(i).wait()
        for i in turns:
            mine = take_columns(2 * i + core, 0)
            other = cols_recv[i]
            lane_at = lax.broadcasted_iota(jnp.int32, mine.shape, 1)
            columns = jnp.where(lane_at < half, mine, other)
            turned = jnp.concatenate(split_bf16(columns), axis=1)
            turned_buf[i] = turned
            high, low = split_bf16(columns.T)
            weight_buf[i, 0:width] = high
            weight_buf[i, width : 2 * width] = low
            demand = mine + pltpu.roll(other, half, 1)
            demand_buf[i] = load_unit * demand.T[half : half + hours]
            pieces = jnp.concatenate(split_bf16(dual_buf[0, i]), axis=0)
            total = total + jnp.dot(pieces, turned, preferred_element_type=jnp.float32)
        return total

    total = lax.fori_loop(
        0, chips // together, collect, jnp.zeros((2 * hours, 2 * width), jnp.float32)
    )

    send_pack.wait()
    state = pack_own[0] + pltpu.roll(pack_sib[0], half, 1)
    energy_dual = pack_own[1] + pltpu.roll(pack_sib[1], half, 1)
    params = pack_own[2] + pltpu.roll(pack_sib[2], half, 1)
    cost, upper, start_energy, energy_limit = (params[r : r + 1] for r in range(4))
    lane = lax.broadcasted_iota(jnp.int32, (hours, width), 1)
    is_gen = lax.rem(lane, half) < units
    lower = jnp.where(is_gen, 0.0, -upper)
    later = running_sum(energy_dual, True)
    own_dual = [dual_buf[0, chip, rows(part)] for part in range(PARTS)]
    state = [state[rows(part)] for part in range(PARTS)]
    is_gen_part, lower_part = is_gen[:part_rows], lower[:part_rows]
    line_max = line_max_ref[...]

    def stacked(values):
        high = values.astype(jnp.bfloat16).astype(jnp.float32)
        return jnp.concatenate([high, values - high], axis=0).astype(jnp.bfloat16)

    def swap_prices(t, part):
        return to_sibling(
            price_send.at[t, rows(part)], price_recv.at[t, rows(part)], price_sem.at[t, part]
        )

    for t in range(ITERS):
        partial = [None] * PARTS
        for part in range(PARTS):
            if t == 0:
                both = total[:hours] + total[hours:]
                both = both[rows(part)]
            else:
                total = jnp.zeros((2 * part_rows, 2 * width), jnp.float32)
                for k in [0] + far_first[::-1]:
                    c = peer(chips - k)
                    if k == 0:
                        dual = own_dual[part]
                    else:
                        recv_dual(t, c, part).wait_recv()
                        dual = dual_buf[t, c, rows(part)]
                    total = total + jnp.dot(
                        stacked(dual), turned_buf[c], preferred_element_type=jnp.float32
                    )
                both = total[:part_rows] + total[part_rows:]
            partial[part] = both[:, :width] + both[:, width:]
            price_send[t, rows(part)] = partial[part]
            swap_prices(t, part).start()

        bars = []
        line_flows = []
        for part in range(PARTS):
            swap_prices(t, part).wait()
            prices = partial[part] + pltpu.roll(price_recv[t, rows(part)], half, 1)
            pull = efficiency * interval * later[rows(part)]
            gradient = jnp.where(is_gen_part, cost + prices, pull - prices)
            step = jnp.clip(state[part] - primal_step * gradient, lower_part, upper)
            bar = 2.0 * step - state[part]
            state[part] = step
            bars.append(bar)
            pieces = stacked(jnp.where(is_gen_part, bar, -bar))
            pieces = jnp.concatenate([pieces, pieces], axis=1)

            def flows(c):
                out = jnp.dot(pieces, weight_buf[c], preferred_element_type=jnp.float32)
                return out[:part_rows] + out[part_rows:] - demand_buf[c, rows(part)]

            for k in far_first:
                flow_send[t, k, rows(part)] = flows(peer(k))
                send_flow(t, k, part).start()
            line_flows.append(flows(chip))

        if t + 1 == ITERS:
            for part in range(PARTS):
                gen_out[rows(part)] = state[part][:, gens]
                charge_out[rows(part)] = state[part][:, stors]
            stores[0].start()
            stores[1].start()
        so_far = running_sum(jnp.concatenate(bars, axis=0), False)
        energy = start_energy + efficiency * interval * so_far
        energy_dual = clip_dual(energy_dual + energy_step * energy, energy_step, 0.0, energy_limit)
        if t + 1 < ITERS:
            later = running_sum(energy_dual, True)
        else:
            energy_out[...] = energy_dual[:, stors]
            stores[2].start()

        for part in range(PARTS):
            flow = line_flows[part]
            for k in far_first[::-1]:
                c = peer(chips - k)
                recv_flow(t, c, part).wait_recv()
                flow = flow + flow_recv[t, c, rows(part)]
            own_dual[part] = clip_dual(
                own_dual[part] + dual_step * flow, dual_step, -line_max, line_max
            )
            if t + 1 < ITERS:
                dual_buf[t + 1, chip, rows(part)] = own_dual[part]
                for k in far_first:
                    send_dual(t + 1, k, part).start()
            else:
                dual_out[rows(part)] = own_dual[part]

    stores[3].start()
    for t in range(ITERS):
        for part in range(PARTS):
            for k in range(1, chips):
                send_dual(t, k, part).wait_send()
                send_flow(t, k, part).wait_send()
    for store in stores:
        store.wait()


def store_kernel(*refs):
    count = len(refs) // 3
    sems = refs[-1]
    fetches = [
        pltpu.make_async_copy(refs[at], refs[2 * count + at], sems.at[0, at]) for at in range(count)
    ]
    stores = [
        pltpu.make_async_copy(refs[2 * count + at], refs[count + at], sems.at[1, at])
        for at in range(count)
    ]
    for fetch in fetches:
        fetch.start()
    for fetch, store in zip(fetches, stores):
        fetch.wait()
        store.start()
    for store in stores:
        store.wait()


def on_device_kernel(
    generation,
    charging,
    flow_dual,
    energy_dual,
    shift_factors,
    load_units,
    generator_bus,
    storage_bus,
    generator_cost,
    generator_max,
    charging_max,
    energy_init,
    energy_max,
    line_max,
):
    lines, buses = shift_factors.shape
    units, hours = generation.shape
    block = flow_dual.shape[0]
    n_bus = lines // block
    chips = n_bus // 2
    half = 2 * units
    width = 2 * half
    hbm = pl.BlockSpec(memory_space=pltpu.HBM)
    f32 = jnp.float32
    dma = pltpu.SemaphoreType.DMA
    arrays = (
        generation.T,
        charging,
        flow_dual.T,
        energy_dual,
        shift_factors,
        load_units.T,
        generator_bus[None, :],
        storage_bus[None, :],
        generator_cost[None, :],
        generator_max[None, :],
        charging_max[None, :],
        energy_init[None, :],
        energy_max[None, :],
        line_max[None, :],
    )
    out_shape = (
        jax.ShapeDtypeStruct((hours, units), f32),
        jax.ShapeDtypeStruct((hours, units), f32),
        jax.ShapeDtypeStruct((hours, block), f32),
        jax.ShapeDtypeStruct((hours, units), f32),
    )
    results = pl.pallas_call(
        functools.partial(iterate_kernel, n_bus),
        out_shape=out_shape,
        in_specs=[hbm] * len(arrays),
        out_specs=(hbm,) * 4,
        scratch_shapes=[
            pltpu.VMEM(array.shape, array.dtype)
            for at, array in enumerate(arrays)
            if at not in (2, 4)
        ]
        + [pltpu.VMEM(result.shape, f32) for result in out_shape]
        + [
            pltpu.VMEM((n_bus, block, buses), f32),
            pltpu.VMEM((2, buses, LANES), jnp.bfloat16),
            pltpu.VMEM((3, hours, width), f32),
            pltpu.VMEM((3, hours, width), f32),
            pltpu.VMEM((chips, block, LANES), f32),
            pltpu.VMEM((chips, block, LANES), f32),
            pltpu.VMEM((chips, 2 * width, block), jnp.bfloat16),
            pltpu.VMEM((chips, block, 2 * width), jnp.bfloat16),
            pltpu.VMEM((chips, hours, block), f32),
            pltpu.VMEM((ITERS, chips, hours, block), f32),
            pltpu.VMEM((ITERS, chips, hours, block), f32),
            pltpu.VMEM((ITERS, chips, hours, block), f32),
            pltpu.VMEM((ITERS, hours, width), f32),
            pltpu.VMEM((ITERS, hours, width), f32),
            dma((len(arrays) - 1,)),
            dma((4,)),
            dma((n_bus,)),
            dma((2,)),
            dma((2, chips)),
            dma((ITERS, PARTS, chips)),
            dma((ITERS, PARTS, chips)),
            dma((ITERS, PARTS, chips)),
            dma((ITERS, PARTS, chips)),
            dma((ITERS, PARTS, 2)),
        ],
        compiler_params=pltpu.CompilerParams(
            collective_id=0, has_side_effects=True, vmem_limit_bytes=VMEM_BYTES
        ),
    )(*arrays)
    gen_new, charge_new, dual_new, energy_new = pl.pallas_call(
        store_kernel,
        out_shape=out_shape,
        in_specs=[hbm] * 4,
        out_specs=(hbm,) * 4,
        scratch_shapes=[pltpu.VMEM(result.shape, f32) for result in out_shape] + [dma((2, 4))],
        compiler_params=pltpu.CompilerParams(vmem_limit_bytes=VMEM_BYTES),
    )(*results)
    return gen_new.T, charge_new, dual_new.T, energy_new


def on_device(
    generation,
    charging,
    flow_dual,
    energy_dual,
    shift_factors,
    load_units,
    generator_bus,
    storage_bus,
    generator_cost,
    generator_max,
    charging_max,
    energy_init,
    energy_max,
    line_max,
):
    bus_local = shift_factors.shape[1]
    gen_local = generator_bus.shape[0]
    stor_local = storage_bus.shape[0]
    own_index = lax.axis_index("bus")
    bus_ids = lax.broadcasted_iota(jnp.int32, (bus_local, 1), 0) + own_index * bus_local
    gen_onehot = (generator_bus[None, :] == bus_ids).astype(jnp.float32)
    stor_onehot = (storage_bus[None, :] == bus_ids).astype(jnp.float32)
    columns = contract(shift_factors, jnp.concatenate([gen_onehot, stor_onehot], axis=1), inner_pair)
    demand = load_units.astype(jnp.float32) * load_unit
    demand_flows = contract(shift_factors, demand, inner_pair)
    unit_cost = generator_cost[:, None]
    ceiling = generator_max[:, None]
    first_slot = own_index * stor_local
    charge_limit = lax.dynamic_slice_in_dim(charging_max, first_slot, stor_local)[None, :]
    start_energy = lax.dynamic_slice_in_dim(energy_init, first_slot, stor_local)[None, :]
    energy_limit = lax.dynamic_slice_in_dim(energy_max, first_slot, stor_local)[None, :]
    for iteration in range(ITERS):
        prices = contract(columns, lax.all_gather(flow_dual, "bus", axis=0, tiled=True), across_first)
        gen_step = jnp.clip(
            generation - primal_step * (unit_cost + prices[:gen_local]), 0.0, ceiling
        )
        gen_bar = 2.0 * gen_step - generation
        stor_prices = prices[gen_local:].T
        gradient = efficiency * interval * reverse_cumsum(energy_dual) - stor_prices
        charge_step = jnp.clip(charging - primal_step * gradient, -charge_limit, charge_limit)
        bar_bus = 2.0 * charge_step - charging
        energy = start_energy + efficiency * interval * jnp.cumsum(bar_bus, axis=0)
        energy_dual = clip_dual(energy_dual + energy_step * energy, energy_step, 0.0, energy_limit)
        charging = charge_step
        bars = jnp.concatenate([gen_bar, -bar_bus.T], axis=0)
        line_flows = lax.psum_scatter(
            contract(columns, bars, inner_pair) - demand_flows, "bus", scatter_dimension=0, tiled=True
        )
        flow_dual = clip_dual(
            flow_dual + dual_step * line_flows, dual_step, -line_max[:, None], line_max[:, None]
        )
        generation = gen_step
    return (generation, charging, flow_dual, energy_dual)


def fits_kernel(n_bus, generation, charging, flow_dual, shift_factors, storage_bus):
    units = generation.shape[0] // n_bus
    stors = storage_bus.shape[0] // n_bus
    block = flow_dual.shape[0] // n_bus
    hours = charging.shape[0] // 2
    buses = shift_factors.shape[1] // n_bus
    return (
        n_bus % 2 == 0
        and units == stors
        and 4 * units == LANES
        and hours == 16
        and block % LANES == 0
        and buses % LANES == 0
        and shift_factors.shape[0] * buses * 4 <= 2**24
    )


def solution(mesh):
    placed = (
        P("bus", "groups"),
        P("groups", "bus"),
        P("bus", "groups"),
        P("groups", "bus"),
        P(None, "bus"),
        P("bus", "groups"),
        P("bus"),
        P("bus"),
        P("bus"),
        P("bus"),
        P(),
        P(),
        P(),
        P("bus"),
    )
    n_bus = mesh.shape["bus"]

    def whole(*arrays):
        fits = mesh.shape["groups"] == 2 and fits_kernel(
            n_bus, arrays[0], arrays[1], arrays[2], arrays[4], arrays[7]
        )
        return jax.shard_map(
            on_device_kernel if fits else on_device,
            mesh=mesh,
            in_specs=placed,
            out_specs=(P("bus", "groups"), P("groups", "bus"), P("bus", "groups"), P("groups", "bus")),
            check_vma=False,
        )(*arrays)

    return whole
```

```python
import functools

import jax
import jax.numpy as jnp
from jax import lax
from jax.experimental import pallas as pl
from jax.experimental.pallas import tpu as pltpu
from jax.sharding import PartitionSpec as P

ITERS = 3
LANES = 128
PARTS = 2
VMEM_BYTES = 65472 * 1024
MESH = pl.DeviceIdType.MESH

primal_step = 0.5
dual_step = 0.5
energy_step = 0.05
efficiency = 0.95
interval = 0.125
load_unit = 0.05
highest = lax.Precision.HIGHEST
across_first = (((0,), (0,)), ((), ()))
across_second = (((1,), (1,)), ((), ()))
inner_pair = (((1,), (0,)), ((), ()))


def contract(left, right, dims):
    return lax.dot_general(left, right, dims, precision=highest, preferred_element_type=jnp.float32)


def reverse_cumsum(values):
    return jnp.flip(jnp.cumsum(jnp.flip(values, 0), axis=0), 0)


def clip_dual(shifted, step_size, low_bound, high_bound):
    return shifted - step_size * jnp.clip(shifted / step_size, low_bound, high_bound)


def split_bf16(values):
    high = values.astype(jnp.bfloat16)
    return high, (values - high.astype(jnp.float32)).astype(jnp.bfloat16)


def running_sum(values, backward):
    rows = values.shape[0]
    row = lax.broadcasted_iota(jnp.int32, values.shape, 0)
    step = 1
    while step < rows:
        if backward:
            moved = jnp.where(row < rows - step, pltpu.roll(values, rows - step, 0), 0.0)
        else:
            moved = jnp.where(row >= step, pltpu.roll(values, step, 0), 0.0)
        values = values + moved
        step *= 2
    return values


def iterate_kernel(
    n_bus,
    gen_hbm,
    charge_hbm,
    dual_hbm,
    energy_hbm,
    factors_hbm,
    load_hbm,
    gen_bus_hbm,
    stor_bus_hbm,
    cost_hbm,
    gen_max_hbm,
    charge_max_hbm,
    init_hbm,
    energy_max_hbm,
    line_max_hbm,
    gen_hbm_out,
    charge_hbm_out,
    dual_hbm_out,
    energy_hbm_out,
    gen_ref,
    charge_ref,
    energy_ref,
    load_ref,
    gen_bus_ref,
    stor_bus_ref,
    cost_ref,
    gen_max_ref,
    charge_max_ref,
    init_ref,
    energy_max_ref,
    line_max_ref,
    gen_out,
    charge_out,
    dual_out,
    energy_out,
    factors_buf,
    place_buf,
    pack_own,
    pack_sib,
    cols_send,
    cols_recv,
    weight_buf,
    turned_buf,
    demand_buf,
    dual_buf,
    flow_send,
    flow_recv,
    price_send,
    price_recv,
    input_sem,
    output_sem,
    factors_sem,
    pack_sem,
    cols_sems,
    dual_send_sem,
    dual_recv_sem,
    flow_send_sem,
    flow_recv_sem,
    price_sem,
):
    chips = n_bus // 2
    hours, units = gen_ref.shape
    block = dual_hbm.shape[1]
    buses = factors_hbm.shape[1]
    half = 2 * units
    width = 2 * half
    me = lax.axis_index("bus")
    core = lax.rem(me, 2)
    chip = lax.div(me, 2)
    sibling = me + 1 - 2 * core
    far_first = sorted(range(1, chips), key=lambda k: abs(2 * k - chips))

    def peer(k):
        return lax.rem(chip + k, chips)

    barrier = pltpu.get_barrier_semaphore()
    for k in range(1, chips):
        pl.semaphore_signal(
            barrier, inc=1, device_id={"bus": 2 * peer(k) + core}, device_id_type=MESH
        )
    pl.semaphore_signal(barrier, inc=1, device_id={"bus": sibling}, device_id_type=MESH)

    dual_in = pltpu.make_async_copy(dual_hbm, dual_buf.at[0, chip], input_sem.at[0])
    fetches = [
        pltpu.make_async_copy(source, target, input_sem.at[1 + at])
        for at, (source, target) in enumerate(
            (
                (load_hbm, load_ref),
                (gen_bus_hbm, gen_bus_ref),
                (stor_bus_hbm, stor_bus_ref),
                (gen_hbm, gen_ref),
                (charge_hbm, charge_ref),
                (energy_hbm, energy_ref),
                (cost_hbm, cost_ref),
                (gen_max_hbm, gen_max_ref),
                (charge_max_hbm, charge_max_ref),
                (init_hbm, init_ref),
                (energy_max_hbm, energy_max_ref),
                (line_max_hbm, line_max_ref),
            )
        )
    ]
    stores = [
        pltpu.make_async_copy(source, target, output_sem.at[at])
        for at, (source, target) in enumerate(
            (
                (gen_out, gen_hbm_out),
                (charge_out, charge_hbm_out),
                (energy_out, energy_hbm_out),
                (dual_out, dual_hbm_out),
            )
        )
    ]
    dual_in.start()
    for fetch in fetches:
        fetch.start()

    def load_factors(slot):
        own = lax.div(slot, chips)
        b = 2 * lax.rem(slot, chips) + lax.rem(core + 1 + own, 2)
        start = pl.multiple_of(b * block, block)
        return pltpu.make_async_copy(
            factors_hbm.at[pl.ds(start, block), :], factors_buf.at[slot], factors_sem.at[slot]
        )

    @pl.loop(0, n_bus)
    def _(slot):
        load_factors(slot).start()

    part_rows = hours // PARTS

    def rows(part):
        return slice(part * part_rows, (part + 1) * part_rows)

    def send_dual(t, k, part):
        return pltpu.make_async_remote_copy(
            src_ref=dual_buf.at[t, chip, rows(part)],
            dst_ref=dual_buf.at[t, chip, rows(part)],
            send_sem=dual_send_sem.at[t, part, k],
            recv_sem=dual_recv_sem.at[t, part, chip],
            device_id={"bus": 2 * peer(k) + core},
            device_id_type=MESH,
        )

    def recv_dual(t, c, part):
        return pltpu.make_async_remote_copy(
            src_ref=dual_buf.at[t, c, rows(part)],
            dst_ref=dual_buf.at[t, c, rows(part)],
            send_sem=dual_send_sem.at[t, part, 0],
            recv_sem=dual_recv_sem.at[t, part, c],
            device_id={"bus": sibling},
            device_id_type=MESH,
        )

    def send_first(k):
        return pltpu.make_async_remote_copy(
            src_ref=dual_buf.at[0, chip],
            dst_ref=dual_buf.at[0, chip],
            send_sem=dual_send_sem.at[0, 0, k],
            recv_sem=dual_recv_sem.at[0, 0, chip],
            device_id={"bus": 2 * peer(k) + core},
            device_id_type=MESH,
        )

    def recv_first(c):
        return pltpu.make_async_remote_copy(
            src_ref=dual_buf.at[0, c],
            dst_ref=dual_buf.at[0, c],
            send_sem=dual_send_sem.at[0, 0, 0],
            recv_sem=dual_recv_sem.at[0, 0, c],
            device_id={"bus": sibling},
            device_id_type=MESH,
        )

    def send_flow(t, k, part):
        return pltpu.make_async_remote_copy(
            src_ref=flow_send.at[t, k, rows(part)],
            dst_ref=flow_recv.at[t, chip, rows(part)],
            send_sem=flow_send_sem.at[t, part, k],
            recv_sem=flow_recv_sem.at[t, part, chip],
            device_id={"bus": 2 * peer(k) + core},
            device_id_type=MESH,
        )

    def recv_flow(t, c, part):
        return pltpu.make_async_remote_copy(
            src_ref=flow_recv.at[t, c, rows(part)],
            dst_ref=flow_recv.at[t, c, rows(part)],
            send_sem=flow_send_sem.at[t, part, 0],
            recv_sem=flow_recv_sem.at[t, part, c],
            device_id={"bus": sibling},
            device_id_type=MESH,
        )

    def to_sibling(source, target, sems):
        return pltpu.make_async_remote_copy(
            src_ref=source,
            dst_ref=target,
            send_sem=sems.at[0],
            recv_sem=sems.at[1],
            device_id={"bus": sibling},
            device_id_type=MESH,
        )

    for fetch in fetches[:3]:
        fetch.wait()
    pack_index = jnp.full((8, LANES), -1, jnp.int32)
    lane8 = lax.broadcasted_iota(jnp.int32, (8, LANES), 1)
    for at, ref in ((0, gen_bus_ref), (units, stor_bus_ref)):
        padded = jnp.concatenate([ref[...], jnp.zeros((1, LANES - units), jnp.int32)], axis=1)
        padded = pltpu.roll(jnp.broadcast_to(padded, (8, LANES)), at, 1)
        pack_index = jnp.where((lane8 >= at) & (lane8 < at + units), padded - me * buses, pack_index)
    bus_id = lax.broadcasted_iota(jnp.int32, (buses, LANES), 0)
    onehot = jnp.where(bus_id == pack_index[0:1, :], 1.0, 0.0)
    loads = jnp.concatenate(
        [
            jnp.zeros((half, buses), jnp.float32),
            load_ref[...].astype(jnp.float32),
            jnp.zeros((LANES - half - hours, buses), jnp.float32),
        ],
        axis=0,
    )
    place = onehot + loads.T
    place_buf[0] = place.astype(jnp.bfloat16)
    place_buf[1] = pltpu.roll(place, half, 1).astype(jnp.bfloat16)

    for fetch in fetches[3:]:
        fetch.wait()
    gens = slice(0, units)
    stors = slice(units, half)
    pack_own[...] = jnp.zeros_like(pack_own)
    pack_own[0, :, gens] = gen_ref[...]
    pack_own[0, :, stors] = charge_ref[...]
    pack_own[1, :, stors] = energy_ref[...]
    pack_own[2, 0:1, gens] = cost_ref[...]
    pack_own[2, 1:2, gens] = gen_max_ref[...]
    first = me * units
    lane_start = pl.multiple_of(lax.div(first, LANES) * LANES, LANES)
    shift = lax.rem(units - lax.rem(first, LANES) + LANES, LANES)
    for row, ref in ((1, charge_max_ref), (2, init_ref), (3, energy_max_ref)):
        chunk = jnp.broadcast_to(ref[0:1, pl.ds(lane_start, LANES)], (8, LANES))
        pack_own[2, row : row + 1, stors] = pltpu.roll(chunk, shift, 1)[0:1, stors]

    pl.semaphore_wait(barrier, chips)
    dual_in.wait()
    for k in far_first:
        send_first(k).start()
    send_pack = to_sibling(pack_own, pack_sib, pack_sem)
    send_pack.start()

    together = 2 if chips % 2 == 0 else 1
    taking = together * block

    def take_columns(slot, placed):
        high, low = split_bf16(factors_buf[pl.ds(slot, together)].reshape(taking, buses))
        taken = jnp.dot(
            jnp.concatenate([high, low], axis=0),
            place_buf[placed],
            preferred_element_type=jnp.float32,
        )
        return taken[:taking] + taken[taking:]

    def swap_columns(i):
        return pltpu.make_async_remote_copy(
            src_ref=cols_send.at[i],
            dst_ref=cols_recv.at[i],
            send_sem=cols_sems.at[0, i],
            recv_sem=cols_sems.at[1, i],
            device_id={"bus": sibling},
            device_id_type=MESH,
        )

    @pl.loop(0, chips // together)
    def _(step):
        turns = [step * together + j for j in range(together)]
        for i in turns:
            load_factors(i).wait()
        taken = take_columns(step * together, 1)
        for j, i in enumerate(turns):
            cols_send[i] = taken[j * block : (j + 1) * block]
            swap_columns(i).start()

    for k in reversed(far_first):
        recv_first(peer(chips - k)).wait_recv()

    def collect(step, total):
        turns = [step * together + j for j in range(together)]
        for i in turns:
            load_factors(chips + i).wait()
        for i in turns:
            swap_columns(i).wait()
        taken = take_columns(chips + step * together, 0)
        for j, i in enumerate(turns):
            mine = taken[j * block : (j + 1) * block]
            other = cols_recv[i]
            lane_at = lax.broadcasted_iota(jnp.int32, mine.shape, 1)
            columns = jnp.where(lane_at < half, mine, other)
            turned = jnp.concatenate(split_bf16(columns), axis=1)
            turned_buf[i] = turned
            high, low = split_bf16(columns.T)
            weight_buf[i, 0:width] = high
            weight_buf[i, width : 2 * width] = low
            demand = mine + pltpu.roll(other, half, 1)
            demand_buf[i] = load_unit * demand.T[half : half + hours]
            pieces = jnp.concatenate(split_bf16(dual_buf[0, i]), axis=0)
            total = total + jnp.dot(pieces, turned, preferred_element_type=jnp.float32)
        return total

    total = lax.fori_loop(
        0, chips // together, collect, jnp.zeros((2 * hours, 2 * width), jnp.float32)
    )
    total = total[:hours] + total[hours:]
    total = total[:, :width] + total[:, width:]

    send_pack.wait()
    state = pack_own[0] + pltpu.roll(pack_sib[0], half, 1)
    energy_dual = pack_own[1] + pltpu.roll(pack_sib[1], half, 1)
    params = pack_own[2] + pltpu.roll(pack_sib[2], half, 1)
    cost, upper, start_energy, energy_limit = (params[r : r + 1] for r in range(4))
    lane = lax.broadcasted_iota(jnp.int32, (hours, width), 1)
    is_gen = lax.rem(lane, half) < units
    lower = jnp.where(is_gen, 0.0, -upper)
    later = running_sum(energy_dual, True)
    own_dual = [dual_buf[0, chip, rows(part)] for part in range(PARTS)]
    state = [state[rows(part)] for part in range(PARTS)]
    is_gen_part, lower_part = is_gen[:part_rows], lower[:part_rows]
    line_max = line_max_ref[...]

    def stacked(values):
        high = values.astype(jnp.bfloat16).astype(jnp.float32)
        return jnp.concatenate([high, values - high], axis=0).astype(jnp.bfloat16)

    def swap_prices(t, part):
        return to_sibling(
            price_send.at[t, rows(part)], price_recv.at[t, rows(part)], price_sem.at[t, part]
        )

    def partial_prices(t, own_dual, part):
        total = jnp.zeros((2 * part_rows, 2 * width), jnp.float32)
        for k in [0] + far_first[::-1]:
            c = peer(chips - k)
            if k == 0:
                dual = own_dual
            else:
                recv_dual(t, c, part).wait_recv()
                dual = dual_buf[t, c, rows(part)]
            total = total + jnp.dot(
                stacked(dual), turned_buf[c], preferred_element_type=jnp.float32
            )
        total = total[:part_rows] + total[part_rows:]
        return total[:, :width] + total[:, width:]

    def offer_prices(t, part, partial):
        price_send[t, rows(part)] = partial
        swap_prices(t, part).start()

    def iterate(t, carry, last):
        state, energy_dual, later, own_dual, partial = carry
        new_state, bars, line_flows = [], [], []
        for part in range(PARTS):
            swap_prices(t, part).wait()
            prices = partial[part] + pltpu.roll(price_recv[t, rows(part)], half, 1)
            pull = efficiency * interval * later[rows(part)]
            gradient = jnp.where(is_gen_part, cost + prices, pull - prices)
            step = jnp.clip(state[part] - primal_step * gradient, lower_part, upper)
            bar = 2.0 * step - state[part]
            new_state.append(step)
            bars.append(bar)
            pieces = stacked(jnp.where(is_gen_part, bar, -bar))
            pieces = jnp.concatenate([pieces, pieces], axis=1)

            def flows(c):
                out = jnp.dot(pieces, weight_buf[c], preferred_element_type=jnp.float32)
                return out[:part_rows] + out[part_rows:] - demand_buf[c, rows(part)]

            for k in far_first:
                flow_send[t, k, rows(part)] = flows(peer(k))
                send_flow(t, k, part).start()
            line_flows.append(flows(chip))

        if last:
            for part in range(PARTS):
                gen_out[rows(part)] = new_state[part][:, gens]
                charge_out[rows(part)] = new_state[part][:, stors]
            stores[0].start()
            stores[1].start()
        so_far = running_sum(jnp.concatenate(bars, axis=0), False)
        energy = start_energy + efficiency * interval * so_far
        energy_dual = clip_dual(energy_dual + energy_step * energy, energy_step, 0.0, energy_limit)
        if last:
            energy_out[...] = energy_dual[:, stors]
            stores[2].start()
        else:
            later = running_sum(energy_dual, True)

        new_dual, new_partial = [], []
        for part in range(PARTS):
            flow = line_flows[part]
            for k in far_first[::-1]:
                c = peer(chips - k)
                recv_flow(t, c, part).wait_recv()
                flow = flow + flow_recv[t, c, rows(part)]
            dual = clip_dual(own_dual[part] + dual_step * flow, dual_step, -line_max, line_max)
            new_dual.append(dual)
            if last:
                dual_out[rows(part)] = dual
            else:
                dual_buf[t + 1, chip, rows(part)] = dual
                for k in far_first:
                    send_dual(t + 1, k, part).start()
        if last:
            stores[3].start()
        else:
            for part in range(PARTS):
                new_partial.append(partial_prices(t + 1, new_dual[part], part))
                offer_prices(t + 1, part, new_partial[part])
        return new_state, energy_dual, later, new_dual, new_partial

    partial = [total[rows(part)] for part in range(PARTS)]
    for part in range(PARTS):
        offer_prices(0, part, partial[part])
    carry = (state, energy_dual, later, own_dual, partial)
    carry = lax.fori_loop(0, ITERS - 1, lambda t, carry: iterate(t, carry, False), carry)
    iterate(ITERS - 1, carry, True)

    for k in range(1, chips):
        send_first(k).wait_send()

    @pl.loop(0, ITERS)
    def _(t):
        for part in range(PARTS):
            for k in range(1, chips):
                send_flow(t, k, part).wait_send()

    @pl.loop(1, ITERS)
    def _(t):
        for part in range(PARTS):
            for k in range(1, chips):
                send_dual(t, k, part).wait_send()

    for store in stores:
        store.wait()


def store_kernel(*refs):
    count = len(refs) // 3
    sems = refs[-1]
    fetches = [
        pltpu.make_async_copy(refs[at], refs[2 * count + at], sems.at[0, at]) for at in range(count)
    ]
    stores = [
        pltpu.make_async_copy(refs[2 * count + at], refs[count + at], sems.at[1, at])
        for at in range(count)
    ]
    for fetch in fetches:
        fetch.start()
    for fetch, store in zip(fetches, stores):
        fetch.wait()
        store.start()
    for store in stores:
        store.wait()


def on_device_kernel(
    generation,
    charging,
    flow_dual,
    energy_dual,
    shift_factors,
    load_units,
    generator_bus,
    storage_bus,
    generator_cost,
    generator_max,
    charging_max,
    energy_init,
    energy_max,
    line_max,
):
    lines, buses = shift_factors.shape
    units, hours = generation.shape
    block = flow_dual.shape[0]
    n_bus = lines // block
    chips = n_bus // 2
    half = 2 * units
    width = 2 * half
    hbm = pl.BlockSpec(memory_space=pltpu.HBM)
    f32 = jnp.float32
    dma = pltpu.SemaphoreType.DMA
    arrays = (
        generation.T,
        charging,
        flow_dual.T,
        energy_dual,
        shift_factors,
        load_units.T,
        generator_bus[None, :],
        storage_bus[None, :],
        generator_cost[None, :],
        generator_max[None, :],
        charging_max[None, :],
        energy_init[None, :],
        energy_max[None, :],
        line_max[None, :],
    )
    out_shape = (
        jax.ShapeDtypeStruct((hours, units), f32),
        jax.ShapeDtypeStruct((hours, units), f32),
        jax.ShapeDtypeStruct((hours, block), f32),
        jax.ShapeDtypeStruct((hours, units), f32),
    )
    results = pl.pallas_call(
        functools.partial(iterate_kernel, n_bus),
        out_shape=out_shape,
        in_specs=[hbm] * len(arrays),
        out_specs=(hbm,) * 4,
        scratch_shapes=[
            pltpu.VMEM(array.shape, array.dtype)
            for at, array in enumerate(arrays)
            if at not in (2, 4)
        ]
        + [pltpu.VMEM(result.shape, f32) for result in out_shape]
        + [
            pltpu.VMEM((n_bus, block, buses), f32),
            pltpu.VMEM((2, buses, LANES), jnp.bfloat16),
            pltpu.VMEM((3, hours, width), f32),
            pltpu.VMEM((3, hours, width), f32),
            pltpu.VMEM((chips, block, LANES), f32),
            pltpu.VMEM((chips, block, LANES), f32),
            pltpu.VMEM((chips, 2 * width, block), jnp.bfloat16),
            pltpu.VMEM((chips, block, 2 * width), jnp.bfloat16),
            pltpu.VMEM((chips, hours, block), f32),
            pltpu.VMEM((ITERS, chips, hours, block), f32),
            pltpu.VMEM((ITERS, chips, hours, block), f32),
            pltpu.VMEM((ITERS, chips, hours, block), f32),
            pltpu.VMEM((ITERS, hours, width), f32),
            pltpu.VMEM((ITERS, hours, width), f32),
            dma((len(arrays) - 1,)),
            dma((4,)),
            dma((n_bus,)),
            dma((2,)),
            dma((2, chips)),
            dma((ITERS, PARTS, chips)),
            dma((ITERS, PARTS, chips)),
            dma((ITERS, PARTS, chips)),
            dma((ITERS, PARTS, chips)),
            dma((ITERS, PARTS, 2)),
        ],
        compiler_params=pltpu.CompilerParams(
            collective_id=0, has_side_effects=True, vmem_limit_bytes=VMEM_BYTES
        ),
    )(*arrays)
    gen_new, charge_new, dual_new, energy_new = pl.pallas_call(
        store_kernel,
        out_shape=out_shape,
        in_specs=[hbm] * 4,
        out_specs=(hbm,) * 4,
        scratch_shapes=[pltpu.VMEM(result.shape, f32) for result in out_shape] + [dma((2, 4))],
        compiler_params=pltpu.CompilerParams(vmem_limit_bytes=VMEM_BYTES),
    )(*results)
    return gen_new.T, charge_new, dual_new.T, energy_new


def on_device(
    generation,
    charging,
    flow_dual,
    energy_dual,
    shift_factors,
    load_units,
    generator_bus,
    storage_bus,
    generator_cost,
    generator_max,
    charging_max,
    energy_init,
    energy_max,
    line_max,
):
    bus_local = shift_factors.shape[1]
    gen_local = generator_bus.shape[0]
    stor_local = storage_bus.shape[0]
    own_index = lax.axis_index("bus")
    bus_ids = lax.broadcasted_iota(jnp.int32, (bus_local, 1), 0) + own_index * bus_local
    gen_onehot = (generator_bus[None, :] == bus_ids).astype(jnp.float32)
    stor_onehot = (storage_bus[None, :] == bus_ids).astype(jnp.float32)
    columns = contract(shift_factors, jnp.concatenate([gen_onehot, stor_onehot], axis=1), inner_pair)
    demand = load_units.astype(jnp.float32) * load_unit
    demand_flows = contract(shift_factors, demand, inner_pair)
    unit_cost = generator_cost[:, None]
    ceiling = generator_max[:, None]
    first_slot = own_index * stor_local
    charge_limit = lax.dynamic_slice_in_dim(charging_max, first_slot, stor_local)[None, :]
    start_energy = lax.dynamic_slice_in_dim(energy_init, first_slot, stor_local)[None, :]
    energy_limit = lax.dynamic_slice_in_dim(energy_max, first_slot, stor_local)[None, :]
    for iteration in range(ITERS):
        prices = contract(columns, lax.all_gather(flow_dual, "bus", axis=0, tiled=True), across_first)
        gen_step = jnp.clip(
            generation - primal_step * (unit_cost + prices[:gen_local]), 0.0, ceiling
        )
        gen_bar = 2.0 * gen_step - generation
        stor_prices = prices[gen_local:].T
        gradient = efficiency * interval * reverse_cumsum(energy_dual) - stor_prices
        charge_step = jnp.clip(charging - primal_step * gradient, -charge_limit, charge_limit)
        bar_bus = 2.0 * charge_step - charging
        energy = start_energy + efficiency * interval * jnp.cumsum(bar_bus, axis=0)
        energy_dual = clip_dual(energy_dual + energy_step * energy, energy_step, 0.0, energy_limit)
        charging = charge_step
        bars = jnp.concatenate([gen_bar, -bar_bus.T], axis=0)
        line_flows = lax.psum_scatter(
            contract(columns, bars, inner_pair) - demand_flows, "bus", scatter_dimension=0, tiled=True
        )
        flow_dual = clip_dual(
            flow_dual + dual_step * line_flows, dual_step, -line_max[:, None], line_max[:, None]
        )
        generation = gen_step
    return (generation, charging, flow_dual, energy_dual)


def fits_kernel(n_bus, generation, charging, flow_dual, shift_factors, storage_bus):
    units = generation.shape[0] // n_bus
    stors = storage_bus.shape[0] // n_bus
    block = flow_dual.shape[0] // n_bus
    hours = charging.shape[0] // 2
    buses = shift_factors.shape[1] // n_bus
    return (
        n_bus % 2 == 0
        and units == stors
        and 4 * units == LANES
        and hours == 16
        and block % LANES == 0
        and buses % LANES == 0
        and shift_factors.shape[0] * buses * 4 <= 2**24
    )


def solution(mesh):
    placed = (
        P("bus", "groups"),
        P("groups", "bus"),
        P("bus", "groups"),
        P("groups", "bus"),
        P(None, "bus"),
        P("bus", "groups"),
        P("bus"),
        P("bus"),
        P("bus"),
        P("bus"),
        P(),
        P(),
        P(),
        P("bus"),
    )
    n_bus = mesh.shape["bus"]

    def whole(*arrays):
        fits = mesh.shape["groups"] == 2 and fits_kernel(
            n_bus, arrays[0], arrays[1], arrays[2], arrays[4], arrays[7]
        )
        return jax.shard_map(
            on_device_kernel if fits else on_device,
            mesh=mesh,
            in_specs=placed,
            out_specs=(P("bus", "groups"), P("groups", "bus"), P("bus", "groups"), P("groups", "bus")),
            check_vma=False,
        )(*arrays)

    return whole
```

```python
import functools

import jax
import jax.numpy as jnp
from jax import lax
from jax.experimental import pallas as pl
from jax.experimental.pallas import tpu as pltpu
from jax.sharding import PartitionSpec as P

ITERS = 3
LANES = 128
PARTS = 2
VMEM_BYTES = 65472 * 1024
MESH = pl.DeviceIdType.MESH

primal_step = 0.5
dual_step = 0.5
energy_step = 0.05
efficiency = 0.95
interval = 0.125
load_unit = 0.05
highest = lax.Precision.HIGHEST
across_first = (((0,), (0,)), ((), ()))
across_second = (((1,), (1,)), ((), ()))
inner_pair = (((1,), (0,)), ((), ()))


def contract(left, right, dims):
    return lax.dot_general(left, right, dims, precision=highest, preferred_element_type=jnp.float32)


def reverse_cumsum(values):
    return jnp.flip(jnp.cumsum(jnp.flip(values, 0), axis=0), 0)


def clip_dual(shifted, step_size, low_bound, high_bound):
    return shifted - step_size * jnp.clip(shifted / step_size, low_bound, high_bound)


def split_bf16(values):
    high = values.astype(jnp.bfloat16)
    return high, (values - high.astype(jnp.float32)).astype(jnp.bfloat16)


def running_sum(values, backward):
    rows = values.shape[0]
    row = lax.broadcasted_iota(jnp.int32, values.shape, 0)
    step = 1
    while step < rows:
        if backward:
            moved = jnp.where(row < rows - step, pltpu.roll(values, rows - step, 0), 0.0)
        else:
            moved = jnp.where(row >= step, pltpu.roll(values, step, 0), 0.0)
        values = values + moved
        step *= 2
    return values


def iterate_kernel(
    n_bus,
    gen_hbm,
    charge_hbm,
    dual_hbm,
    energy_hbm,
    factors_hbm,
    load_hbm,
    gen_bus_hbm,
    stor_bus_hbm,
    cost_hbm,
    gen_max_hbm,
    charge_max_hbm,
    init_hbm,
    energy_max_hbm,
    line_max_hbm,
    gen_hbm_out,
    charge_hbm_out,
    dual_hbm_out,
    energy_hbm_out,
    gen_ref,
    charge_ref,
    energy_ref,
    load_ref,
    gen_bus_ref,
    stor_bus_ref,
    cost_ref,
    gen_max_ref,
    charge_max_ref,
    init_ref,
    energy_max_ref,
    line_max_ref,
    gen_out,
    charge_out,
    dual_out,
    energy_out,
    factors_buf,
    place_buf,
    pack_own,
    pack_sib,
    cols_send,
    cols_recv,
    weight_buf,
    turned_buf,
    demand_buf,
    dual_buf,
    across_send,
    across_recv,
    flow_send,
    flow_recv,
    price_send,
    price_recv,
    input_sem,
    output_sem,
    factors_sem,
    pack_sem,
    cols_sems,
    first_sem,
    dual_send_sem,
    dual_recv_sem,
    dual_across_sem,
    flow_send_sem,
    flow_recv_sem,
    flow_across_sem,
    price_sem,
):
    chips = n_bus // 2
    hours, units = gen_ref.shape
    block = dual_hbm.shape[1]
    buses = factors_hbm.shape[1]
    half = 2 * units
    width = 2 * half
    me = lax.axis_index("bus")
    core = lax.rem(me, 2)
    chip = lax.div(me, 2)
    sibling = me + 1 - 2 * core
    far_first = sorted(range(1, chips), key=lambda k: abs(2 * k - chips))
    depth = chips // 2
    row = lax.rem(chip, 2)
    place_z = lax.div(chip, 2)
    across = 2 * (chip + 1 - 2 * row) + core
    far_z = sorted(range(1, depth), key=lambda k: abs(2 * k - depth))

    def peer_z(k):
        return lax.rem(place_z + k, depth)

    def device_z(k):
        return 2 * (2 * peer_z(k) + row) + core

    def peer(k):
        return lax.rem(chip + k, chips)

    barrier = pltpu.get_barrier_semaphore()
    for k in range(1, chips):
        pl.semaphore_signal(
            barrier, inc=1, device_id={"bus": 2 * peer(k) + core}, device_id_type=MESH
        )
    pl.semaphore_signal(barrier, inc=1, device_id={"bus": sibling}, device_id_type=MESH)

    dual_in = pltpu.make_async_copy(dual_hbm, dual_buf.at[0, row, place_z], input_sem.at[0])
    fetches = [
        pltpu.make_async_copy(source, target, input_sem.at[1 + at])
        for at, (source, target) in enumerate(
            (
                (load_hbm, load_ref),
                (gen_bus_hbm, gen_bus_ref),
                (stor_bus_hbm, stor_bus_ref),
                (gen_hbm, gen_ref),
                (charge_hbm, charge_ref),
                (energy_hbm, energy_ref),
                (cost_hbm, cost_ref),
                (gen_max_hbm, gen_max_ref),
                (charge_max_hbm, charge_max_ref),
                (init_hbm, init_ref),
                (energy_max_hbm, energy_max_ref),
                (line_max_hbm, line_max_ref),
            )
        )
    ]
    stores = [
        pltpu.make_async_copy(source, target, output_sem.at[at])
        for at, (source, target) in enumerate(
            (
                (gen_out, gen_hbm_out),
                (charge_out, charge_hbm_out),
                (energy_out, energy_hbm_out),
                (dual_out, dual_hbm_out),
            )
        )
    ]
    dual_in.start()
    for fetch in fetches:
        fetch.start()

    def load_factors(slot):
        own = lax.div(slot, chips)
        b = 2 * lax.rem(slot, chips) + lax.rem(core + 1 + own, 2)
        start = pl.multiple_of(b * block, block)
        return pltpu.make_async_copy(
            factors_hbm.at[pl.ds(start, block), :], factors_buf.at[slot], factors_sem.at[slot]
        )

    @pl.loop(0, n_bus)
    def _(slot):
        load_factors(slot).start()

    part_rows = hours // PARTS

    def rows(part):
        return slice(part * part_rows, (part + 1) * part_rows)

    def remote(source, target, sent, received, device):
        return pltpu.make_async_remote_copy(
            src_ref=source,
            dst_ref=target,
            send_sem=sent,
            recv_sem=received,
            device_id={"bus": device},
            device_id_type=MESH,
        )

    def send_first(k):
        own = dual_buf.at[0, row, place_z]
        return remote(
            own, own, first_sem.at[0, k], first_sem.at[1, chip], 2 * peer(k) + core
        )

    def recv_first(c):
        slot = dual_buf.at[0, lax.rem(c, 2), lax.div(c, 2)]
        return remote(slot, slot, first_sem.at[0, 0], first_sem.at[1, c], sibling)

    def send_dual(t, k, part):
        own = dual_buf.at[t, row, place_z, rows(part)]
        return remote(
            own,
            own,
            dual_send_sem.at[t, part, k],
            dual_recv_sem.at[t, part, place_z],
            device_z(k),
        )

    def recv_dual(t, z, part):
        slot = dual_buf.at[t, row, z, rows(part)]
        return remote(
            slot, slot, dual_send_sem.at[t, part, 0], dual_recv_sem.at[t, part, z], sibling
        )

    def pass_duals(t, part):
        line = dual_buf.at[t, row, :, rows(part)]
        return remote(
            line, line, dual_across_sem.at[t, part, 0], dual_across_sem.at[t, part, 1], across
        )

    def pass_flows(t, part):
        return remote(
            across_send.at[t, :, rows(part)],
            across_recv.at[t, :, rows(part)],
            flow_across_sem.at[t, part, 0],
            flow_across_sem.at[t, part, 1],
            across,
        )

    def send_flow(t, k, part):
        return remote(
            flow_send.at[t, k, rows(part)],
            flow_recv.at[t, place_z, rows(part)],
            flow_send_sem.at[t, part, k],
            flow_recv_sem.at[t, part, place_z],
            device_z(k),
        )

    def recv_flow(t, z, part):
        slot = flow_recv.at[t, z, rows(part)]
        return remote(
            slot, slot, flow_send_sem.at[t, part, 0], flow_recv_sem.at[t, part, z], sibling
        )

    def to_sibling(source, target, sems):
        return pltpu.make_async_remote_copy(
            src_ref=source,
            dst_ref=target,
            send_sem=sems.at[0],
            recv_sem=sems.at[1],
            device_id={"bus": sibling},
            device_id_type=MESH,
        )

    for fetch in fetches[:3]:
        fetch.wait()
    pack_index = jnp.full((8, LANES), -1, jnp.int32)
    lane8 = lax.broadcasted_iota(jnp.int32, (8, LANES), 1)
    for at, ref in ((0, gen_bus_ref), (units, stor_bus_ref)):
        padded = jnp.concatenate([ref[...], jnp.zeros((1, LANES - units), jnp.int32)], axis=1)
        padded = pltpu.roll(jnp.broadcast_to(padded, (8, LANES)), at, 1)
        pack_index = jnp.where((lane8 >= at) & (lane8 < at + units), padded - me * buses, pack_index)
    bus_id = lax.broadcasted_iota(jnp.int32, (buses, LANES), 0)
    onehot = jnp.where(bus_id == pack_index[0:1, :], 1.0, 0.0)
    loads = jnp.concatenate(
        [
            jnp.zeros((half, buses), jnp.float32),
            load_ref[...].astype(jnp.float32),
            jnp.zeros((LANES - half - hours, buses), jnp.float32),
        ],
        axis=0,
    )
    place = onehot + loads.T
    place_buf[0] = place.astype(jnp.bfloat16)
    place_buf[1] = pltpu.roll(place, half, 1).astype(jnp.bfloat16)

    for fetch in fetches[3:]:
        fetch.wait()
    gens = slice(0, units)
    stors = slice(units, half)
    pack_own[...] = jnp.zeros_like(pack_own)
    pack_own[0, :, gens] = gen_ref[...]
    pack_own[0, :, stors] = charge_ref[...]
    pack_own[1, :, stors] = energy_ref[...]
    pack_own[2, 0:1, gens] = cost_ref[...]
    pack_own[2, 1:2, gens] = gen_max_ref[...]
    first = me * units
    lane_start = pl.multiple_of(lax.div(first, LANES) * LANES, LANES)
    shift = lax.rem(units - lax.rem(first, LANES) + LANES, LANES)
    for param, ref in ((1, charge_max_ref), (2, init_ref), (3, energy_max_ref)):
        chunk = jnp.broadcast_to(ref[0:1, pl.ds(lane_start, LANES)], (8, LANES))
        pack_own[2, param : param + 1, stors] = pltpu.roll(chunk, shift, 1)[0:1, stors]

    pl.semaphore_wait(barrier, chips)
    dual_in.wait()
    for k in far_first:
        send_first(k).start()
    send_pack = to_sibling(pack_own, pack_sib, pack_sem)
    send_pack.start()

    together = 2 if chips % 2 == 0 else 1
    taking = together * block

    def take_columns(slot, placed):
        high, low = split_bf16(factors_buf[pl.ds(slot, together)].reshape(taking, buses))
        taken = jnp.dot(
            jnp.concatenate([high, low], axis=0),
            place_buf[placed],
            preferred_element_type=jnp.float32,
        )
        return taken[:taking] + taken[taking:]

    def swap_columns(i):
        return pltpu.make_async_remote_copy(
            src_ref=cols_send.at[i],
            dst_ref=cols_recv.at[i],
            send_sem=cols_sems.at[0, i],
            recv_sem=cols_sems.at[1, i],
            device_id={"bus": sibling},
            device_id_type=MESH,
        )

    @pl.loop(0, chips // together)
    def _(step):
        turns = [step * together + j for j in range(together)]
        for i in turns:
            load_factors(i).wait()
        taken = take_columns(step * together, 1)
        for j, i in enumerate(turns):
            cols_send[i] = taken[j * block : (j + 1) * block]
            swap_columns(i).start()

    for k in reversed(far_first):
        recv_first(peer(chips - k)).wait_recv()

    def collect(step, total):
        turns = [step * together + j for j in range(together)]
        for i in turns:
            load_factors(chips + i).wait()
        for i in turns:
            swap_columns(i).wait()
        taken = take_columns(chips + step * together, 0)
        for j, i in enumerate(turns):
            mine = taken[j * block : (j + 1) * block]
            other = cols_recv[i]
            lane_at = lax.broadcasted_iota(jnp.int32, mine.shape, 1)
            columns = jnp.where(lane_at < half, mine, other)
            turned = jnp.concatenate(split_bf16(columns), axis=1)
            turned_buf[i] = turned
            high, low = split_bf16(columns.T)
            weight_buf[i, 0:width] = high
            weight_buf[i, width : 2 * width] = low
            demand = mine + pltpu.roll(other, half, 1)
            demand_buf[i] = load_unit * demand.T[half : half + hours]
            first_dual = dual_buf[0, lax.rem(i, 2), lax.div(i, 2)]
            pieces = jnp.concatenate(split_bf16(first_dual), axis=0)
            total = total + jnp.dot(pieces, turned, preferred_element_type=jnp.float32)
        return total

    total = lax.fori_loop(
        0, chips // together, collect, jnp.zeros((2 * hours, 2 * width), jnp.float32)
    )
    total = total[:hours] + total[hours:]
    total = total[:, :width] + total[:, width:]

    send_pack.wait()
    state = pack_own[0] + pltpu.roll(pack_sib[0], half, 1)
    energy_dual = pack_own[1] + pltpu.roll(pack_sib[1], half, 1)
    params = pack_own[2] + pltpu.roll(pack_sib[2], half, 1)
    cost, upper, start_energy, energy_limit = (params[r : r + 1] for r in range(4))
    lane = lax.broadcasted_iota(jnp.int32, (hours, width), 1)
    is_gen = lax.rem(lane, half) < units
    lower = jnp.where(is_gen, 0.0, -upper)
    later = running_sum(energy_dual, True)
    own_dual = [dual_buf[0, row, place_z, rows(part)] for part in range(PARTS)]
    state = [state[rows(part)] for part in range(PARTS)]
    is_gen_part, lower_part = is_gen[:part_rows], lower[:part_rows]
    line_max = line_max_ref[...]

    def stacked(values):
        high = values.astype(jnp.bfloat16).astype(jnp.float32)
        return jnp.concatenate([high, values - high], axis=0).astype(jnp.bfloat16)

    def swap_prices(t, part):
        return to_sibling(
            price_send.at[t, rows(part)], price_recv.at[t, rows(part)], price_sem.at[t, part]
        )

    def price_term(dual, c):
        return jnp.dot(stacked(dual), turned_buf[c], preferred_element_type=jnp.float32)

    def folded(total):
        total = total[:part_rows] + total[part_rows:]
        return total[:, :width] + total[:, width:]

    def offer_prices(t, part, partial):
        price_send[t, rows(part)] = partial
        swap_prices(t, part).start()

    def iterate(t, carry, last):
        state, energy_dual, later, own_dual, partial = carry
        new_state, bars, line_flows = [], [], []
        for part in range(PARTS):
            swap_prices(t, part).wait()
            prices = partial[part] + pltpu.roll(price_recv[t, rows(part)], half, 1)
            pull = efficiency * interval * later[rows(part)]
            gradient = jnp.where(is_gen_part, cost + prices, pull - prices)
            step = jnp.clip(state[part] - primal_step * gradient, lower_part, upper)
            bar = 2.0 * step - state[part]
            new_state.append(step)
            bars.append(bar)
            pieces = stacked(jnp.where(is_gen_part, bar, -bar))
            pieces = jnp.concatenate([pieces, pieces], axis=1)

            def flows(c):
                out = jnp.dot(pieces, weight_buf[c], preferred_element_type=jnp.float32)
                return out[:part_rows] + out[part_rows:] - demand_buf[c, rows(part)]

            for z in range(depth):
                across_send[t, z, rows(part)] = flows(2 * z + 1 - row)
            pass_flows(t, part).start()
            line_flows.append({k: flows(2 * peer_z(k) + row) for k in far_z + [0]})

        for part in range(PARTS):
            pass_flows(t, part).wait_recv()
            for k in far_z:
                arrived = across_recv[t, peer_z(k), rows(part)]
                flow_send[t, k, rows(part)] = line_flows[part][k] + arrived
                send_flow(t, k, part).start()
            line_flows[part] = line_flows[part][0] + across_recv[t, place_z, rows(part)]

        if last:
            for part in range(PARTS):
                gen_out[rows(part)] = new_state[part][:, gens]
                charge_out[rows(part)] = new_state[part][:, stors]
            stores[0].start()
            stores[1].start()
        so_far = running_sum(jnp.concatenate(bars, axis=0), False)
        energy = start_energy + efficiency * interval * so_far
        energy_dual = clip_dual(energy_dual + energy_step * energy, energy_step, 0.0, energy_limit)
        if last:
            energy_out[...] = energy_dual[:, stors]
            stores[2].start()
        else:
            later = running_sum(energy_dual, True)

        new_dual, new_partial = [], []
        for part in range(PARTS):
            flow = line_flows[part]
            for k in far_z[::-1]:
                z = peer_z(depth - k)
                recv_flow(t, z, part).wait_recv()
                flow = flow + flow_recv[t, z, rows(part)]
            dual = clip_dual(own_dual[part] + dual_step * flow, dual_step, -line_max, line_max)
            new_dual.append(dual)
            if last:
                dual_out[rows(part)] = dual
            else:
                dual_buf[t + 1, row, place_z, rows(part)] = dual
                for k in far_z:
                    send_dual(t + 1, k, part).start()
        if last:
            stores[3].start()
        else:
            totals = []
            for part in range(PARTS):
                for k in far_z[::-1]:
                    recv_dual(t + 1, peer_z(depth - k), part).wait_recv()
                pass_duals(t + 1, part).start()
                total = jnp.zeros((2 * part_rows, 2 * width), jnp.float32)
                for z in range(depth):
                    dual = dual_buf[t + 1, row, z, rows(part)]
                    total = total + price_term(dual, 2 * z + row)
                totals.append(total)
            for part in range(PARTS):
                pass_duals(t + 1, part).wait_recv()
                total = totals[part]
                for z in range(depth):
                    dual = dual_buf[t + 1, 1 - row, z, rows(part)]
                    total = total + price_term(dual, 2 * z + 1 - row)
                new_partial.append(folded(total))
                offer_prices(t + 1, part, new_partial[part])
        return new_state, energy_dual, later, new_dual, new_partial

    partial = [total[rows(part)] for part in range(PARTS)]
    for part in range(PARTS):
        offer_prices(0, part, partial[part])
    carry = (state, energy_dual, later, own_dual, partial)
    carry = lax.fori_loop(0, ITERS - 1, lambda t, carry: iterate(t, carry, False), carry)
    iterate(ITERS - 1, carry, True)

    for k in range(1, chips):
        send_first(k).wait_send()

    @pl.loop(0, ITERS)
    def _(t):
        for part in range(PARTS):
            pass_flows(t, part).wait_send()
            for k in range(1, depth):
                send_flow(t, k, part).wait_send()

    @pl.loop(1, ITERS)
    def _(t):
        for part in range(PARTS):
            pass_duals(t, part).wait_send()
            for k in range(1, depth):
                send_dual(t, k, part).wait_send()

    for store in stores:
        store.wait()


def store_kernel(*refs):
    count = len(refs) // 3
    sems = refs[-1]
    fetches = [
        pltpu.make_async_copy(refs[at], refs[2 * count + at], sems.at[0, at]) for at in range(count)
    ]
    stores = [
        pltpu.make_async_copy(refs[2 * count + at], refs[count + at], sems.at[1, at])
        for at in range(count)
    ]
    for fetch in fetches:
        fetch.start()
    for fetch, store in zip(fetches, stores):
        fetch.wait()
        store.start()
    for store in stores:
        store.wait()


def on_device_kernel(
    generation,
    charging,
    flow_dual,
    energy_dual,
    shift_factors,
    load_units,
    generator_bus,
    storage_bus,
    generator_cost,
    generator_max,
    charging_max,
    energy_init,
    energy_max,
    line_max,
):
    lines, buses = shift_factors.shape
    units, hours = generation.shape
    block = flow_dual.shape[0]
    n_bus = lines // block
    chips = n_bus // 2
    depth = chips // 2
    half = 2 * units
    width = 2 * half
    hbm = pl.BlockSpec(memory_space=pltpu.HBM)
    f32 = jnp.float32
    dma = pltpu.SemaphoreType.DMA
    arrays = (
        generation.T,
        charging,
        flow_dual.T,
        energy_dual,
        shift_factors,
        load_units.T,
        generator_bus[None, :],
        storage_bus[None, :],
        generator_cost[None, :],
        generator_max[None, :],
        charging_max[None, :],
        energy_init[None, :],
        energy_max[None, :],
        line_max[None, :],
    )
    out_shape = (
        jax.ShapeDtypeStruct((hours, units), f32),
        jax.ShapeDtypeStruct((hours, units), f32),
        jax.ShapeDtypeStruct((hours, block), f32),
        jax.ShapeDtypeStruct((hours, units), f32),
    )
    results = pl.pallas_call(
        functools.partial(iterate_kernel, n_bus),
        out_shape=out_shape,
        in_specs=[hbm] * len(arrays),
        out_specs=(hbm,) * 4,
        scratch_shapes=[
            pltpu.VMEM(array.shape, array.dtype)
            for at, array in enumerate(arrays)
            if at not in (2, 4)
        ]
        + [pltpu.VMEM(result.shape, f32) for result in out_shape]
        + [
            pltpu.VMEM((n_bus, block, buses), f32),
            pltpu.VMEM((2, buses, LANES), jnp.bfloat16),
            pltpu.VMEM((3, hours, width), f32),
            pltpu.VMEM((3, hours, width), f32),
            pltpu.VMEM((chips, block, LANES), f32),
            pltpu.VMEM((chips, block, LANES), f32),
            pltpu.VMEM((chips, 2 * width, block), jnp.bfloat16),
            pltpu.VMEM((chips, block, 2 * width), jnp.bfloat16),
            pltpu.VMEM((chips, hours, block), f32),
            pltpu.VMEM((ITERS, 2, depth, hours, block), f32),
            pltpu.VMEM((ITERS, depth, hours, block), f32),
            pltpu.VMEM((ITERS, depth, hours, block), f32),
            pltpu.VMEM((ITERS, depth, hours, block), f32),
            pltpu.VMEM((ITERS, depth, hours, block), f32),
            pltpu.VMEM((ITERS, hours, width), f32),
            pltpu.VMEM((ITERS, hours, width), f32),
            dma((len(arrays) - 1,)),
            dma((4,)),
            dma((n_bus,)),
            dma((2,)),
            dma((2, chips)),
            dma((2, chips)),
            dma((ITERS, PARTS, depth)),
            dma((ITERS, PARTS, depth)),
            dma((ITERS, PARTS, 2)),
            dma((ITERS, PARTS, depth)),
            dma((ITERS, PARTS, depth)),
            dma((ITERS, PARTS, 2)),
            dma((ITERS, PARTS, 2)),
        ],
        compiler_params=pltpu.CompilerParams(
            collective_id=0, has_side_effects=True, vmem_limit_bytes=VMEM_BYTES
        ),
    )(*arrays)
    gen_new, charge_new, dual_new, energy_new = pl.pallas_call(
        store_kernel,
        out_shape=out_shape,
        in_specs=[hbm] * 4,
        out_specs=(hbm,) * 4,
        scratch_shapes=[pltpu.VMEM(result.shape, f32) for result in out_shape] + [dma((2, 4))],
        compiler_params=pltpu.CompilerParams(vmem_limit_bytes=VMEM_BYTES),
    )(*results)
    return gen_new.T, charge_new, dual_new.T, energy_new


def on_device(
    generation,
    charging,
    flow_dual,
    energy_dual,
    shift_factors,
    load_units,
    generator_bus,
    storage_bus,
    generator_cost,
    generator_max,
    charging_max,
    energy_init,
    energy_max,
    line_max,
):
    bus_local = shift_factors.shape[1]
    gen_local = generator_bus.shape[0]
    stor_local = storage_bus.shape[0]
    own_index = lax.axis_index("bus")
    bus_ids = lax.broadcasted_iota(jnp.int32, (bus_local, 1), 0) + own_index * bus_local
    gen_onehot = (generator_bus[None, :] == bus_ids).astype(jnp.float32)
    stor_onehot = (storage_bus[None, :] == bus_ids).astype(jnp.float32)
    columns = contract(shift_factors, jnp.concatenate([gen_onehot, stor_onehot], axis=1), inner_pair)
    demand = load_units.astype(jnp.float32) * load_unit
    demand_flows = contract(shift_factors, demand, inner_pair)
    unit_cost = generator_cost[:, None]
    ceiling = generator_max[:, None]
    first_slot = own_index * stor_local
    charge_limit = lax.dynamic_slice_in_dim(charging_max, first_slot, stor_local)[None, :]
    start_energy = lax.dynamic_slice_in_dim(energy_init, first_slot, stor_local)[None, :]
    energy_limit = lax.dynamic_slice_in_dim(energy_max, first_slot, stor_local)[None, :]
    for iteration in range(ITERS):
        prices = contract(columns, lax.all_gather(flow_dual, "bus", axis=0, tiled=True), across_first)
        gen_step = jnp.clip(
            generation - primal_step * (unit_cost + prices[:gen_local]), 0.0, ceiling
        )
        gen_bar = 2.0 * gen_step - generation
        stor_prices = prices[gen_local:].T
        gradient = efficiency * interval * reverse_cumsum(energy_dual) - stor_prices
        charge_step = jnp.clip(charging - primal_step * gradient, -charge_limit, charge_limit)
        bar_bus = 2.0 * charge_step - charging
        energy = start_energy + efficiency * interval * jnp.cumsum(bar_bus, axis=0)
        energy_dual = clip_dual(energy_dual + energy_step * energy, energy_step, 0.0, energy_limit)
        charging = charge_step
        bars = jnp.concatenate([gen_bar, -bar_bus.T], axis=0)
        line_flows = lax.psum_scatter(
            contract(columns, bars, inner_pair) - demand_flows, "bus", scatter_dimension=0, tiled=True
        )
        flow_dual = clip_dual(
            flow_dual + dual_step * line_flows, dual_step, -line_max[:, None], line_max[:, None]
        )
        generation = gen_step
    return (generation, charging, flow_dual, energy_dual)


def fits_kernel(n_bus, generation, charging, flow_dual, shift_factors, storage_bus):
    units = generation.shape[0] // n_bus
    stors = storage_bus.shape[0] // n_bus
    block = flow_dual.shape[0] // n_bus
    hours = charging.shape[0] // 2
    buses = shift_factors.shape[1] // n_bus
    return (
        n_bus % 4 == 0
        and units == stors
        and 4 * units == LANES
        and hours == 16
        and block % LANES == 0
        and buses % LANES == 0
        and shift_factors.shape[0] * buses * 4 <= 2**24
    )


def solution(mesh):
    placed = (
        P("bus", "groups"),
        P("groups", "bus"),
        P("bus", "groups"),
        P("groups", "bus"),
        P(None, "bus"),
        P("bus", "groups"),
        P("bus"),
        P("bus"),
        P("bus"),
        P("bus"),
        P(),
        P(),
        P(),
        P("bus"),
    )
    n_bus = mesh.shape["bus"]

    def whole(*arrays):
        fits = mesh.shape["groups"] == 2 and fits_kernel(
            n_bus, arrays[0], arrays[1], arrays[2], arrays[4], arrays[7]
        )
        return jax.shard_map(
            on_device_kernel if fits else on_device,
            mesh=mesh,
            in_specs=placed,
            out_specs=(P("bus", "groups"), P("groups", "bus"), P("bus", "groups"), P("groups", "bus")),
            check_vma=False,
        )(*arrays)

    return whole
```

```python
import functools

import jax
import jax.numpy as jnp
from jax import lax
from jax.experimental import pallas as pl
from jax.experimental.pallas import tpu as pltpu
from jax.sharding import PartitionSpec as P

ITERS = 3
LANES = 128
PARTS = 2
VMEM_BYTES = 65472 * 1024
MESH = pl.DeviceIdType.MESH

primal_step = 0.5
dual_step = 0.5
energy_step = 0.05
efficiency = 0.95
interval = 0.125
load_unit = 0.05
highest = lax.Precision.HIGHEST
across_first = (((0,), (0,)), ((), ()))
across_second = (((1,), (1,)), ((), ()))
inner_pair = (((1,), (0,)), ((), ()))


def contract(left, right, dims):
    return lax.dot_general(left, right, dims, precision=highest, preferred_element_type=jnp.float32)


def reverse_cumsum(values):
    return jnp.flip(jnp.cumsum(jnp.flip(values, 0), axis=0), 0)


def clip_dual(shifted, step_size, low_bound, high_bound):
    return shifted - step_size * jnp.clip(shifted / step_size, low_bound, high_bound)


def split_bf16(values):
    high = values.astype(jnp.bfloat16)
    return high, (values - high.astype(jnp.float32)).astype(jnp.bfloat16)


def running_sum(values, backward):
    rows = values.shape[0]
    row = lax.broadcasted_iota(jnp.int32, values.shape, 0)
    step = 1
    while step < rows:
        if backward:
            moved = jnp.where(row < rows - step, pltpu.roll(values, rows - step, 0), 0.0)
        else:
            moved = jnp.where(row >= step, pltpu.roll(values, step, 0), 0.0)
        values = values + moved
        step *= 2
    return values


def iterate_kernel(
    n_bus,
    gen_hbm,
    charge_hbm,
    dual_hbm,
    energy_hbm,
    factors_hbm,
    load_hbm,
    gen_bus_hbm,
    stor_bus_hbm,
    cost_hbm,
    gen_max_hbm,
    charge_max_hbm,
    init_hbm,
    energy_max_hbm,
    line_max_hbm,
    gen_hbm_out,
    charge_hbm_out,
    dual_hbm_out,
    energy_hbm_out,
    gen_ref,
    charge_ref,
    energy_ref,
    load_ref,
    gen_bus_ref,
    stor_bus_ref,
    cost_ref,
    gen_max_ref,
    charge_max_ref,
    init_ref,
    energy_max_ref,
    line_max_ref,
    gen_out,
    charge_out,
    dual_out,
    energy_out,
    factors_buf,
    place_buf,
    pack_own,
    pack_sib,
    cols_send,
    cols_recv,
    weight_buf,
    turned_buf,
    demand_buf,
    dual_buf,
    flow_send,
    flow_recv,
    price_send,
    price_recv,
    input_sem,
    output_sem,
    factors_sem,
    pack_sem,
    cols_sems,
    dual_send_sem,
    dual_recv_sem,
    flow_send_sem,
    flow_recv_sem,
    price_sem,
):
    chips = n_bus // 2
    hours, units = gen_ref.shape
    block = dual_hbm.shape[1]
    buses = factors_hbm.shape[1]
    half = 2 * units
    width = 2 * half
    me = lax.axis_index("bus")
    core = lax.rem(me, 2)
    chip = lax.div(me, 2)
    sibling = me + 1 - 2 * core
    far_first = sorted(range(1, chips), key=lambda k: abs(2 * k - chips))

    def peer(k):
        return lax.rem(chip + k, chips)

    barrier = pltpu.get_barrier_semaphore()
    for k in range(1, chips):
        pl.semaphore_signal(
            barrier, inc=1, device_id={"bus": 2 * peer(k) + core}, device_id_type=MESH
        )
    pl.semaphore_signal(barrier, inc=1, device_id={"bus": sibling}, device_id_type=MESH)

    dual_in = pltpu.make_async_copy(dual_hbm, dual_buf.at[0, chip], input_sem.at[0])
    fetches = [
        pltpu.make_async_copy(source, target, input_sem.at[1 + at])
        for at, (source, target) in enumerate(
            (
                (load_hbm, load_ref),
                (gen_bus_hbm, gen_bus_ref),
                (stor_bus_hbm, stor_bus_ref),
                (gen_hbm, gen_ref),
                (charge_hbm, charge_ref),
                (energy_hbm, energy_ref),
                (cost_hbm, cost_ref),
                (gen_max_hbm, gen_max_ref),
                (charge_max_hbm, charge_max_ref),
                (init_hbm, init_ref),
                (energy_max_hbm, energy_max_ref),
                (line_max_hbm, line_max_ref),
            )
        )
    ]
    stores = [
        pltpu.make_async_copy(source, target, output_sem.at[at])
        for at, (source, target) in enumerate(
            (
                (gen_out, gen_hbm_out),
                (charge_out, charge_hbm_out),
                (energy_out, energy_hbm_out),
                (dual_out, dual_hbm_out),
            )
        )
    ]
    dual_in.start()
    for fetch in fetches:
        fetch.start()

    def load_factors(slot):
        own = lax.div(slot, chips)
        b = 2 * lax.rem(slot, chips) + lax.rem(core + 1 + own, 2)
        start = pl.multiple_of(b * block, block)
        return pltpu.make_async_copy(
            factors_hbm.at[pl.ds(start, block), :], factors_buf.at[slot], factors_sem.at[slot]
        )

    @pl.loop(0, n_bus)
    def _(slot):
        load_factors(slot).start()

    part_rows = hours // PARTS

    def rows(part):
        return slice(part * part_rows, (part + 1) * part_rows)

    def send_dual(t, k, part):
        return pltpu.make_async_remote_copy(
            src_ref=dual_buf.at[t, chip, rows(part)],
            dst_ref=dual_buf.at[t, chip, rows(part)],
            send_sem=dual_send_sem.at[t, part, k],
            recv_sem=dual_recv_sem.at[t, part, chip],
            device_id={"bus": 2 * peer(k) + core},
            device_id_type=MESH,
        )

    def recv_dual(t, c, part):
        return pltpu.make_async_remote_copy(
            src_ref=dual_buf.at[t, c, rows(part)],
            dst_ref=dual_buf.at[t, c, rows(part)],
            send_sem=dual_send_sem.at[t, part, 0],
            recv_sem=dual_recv_sem.at[t, part, c],
            device_id={"bus": sibling},
            device_id_type=MESH,
        )

    def send_first(k):
        return pltpu.make_async_remote_copy(
            src_ref=dual_buf.at[0, chip],
            dst_ref=dual_buf.at[0, chip],
            send_sem=dual_send_sem.at[0, 0, k],
            recv_sem=dual_recv_sem.at[0, 0, chip],
            device_id={"bus": 2 * peer(k) + core},
            device_id_type=MESH,
        )

    def recv_first(c):
        return pltpu.make_async_remote_copy(
            src_ref=dual_buf.at[0, c],
            dst_ref=dual_buf.at[0, c],
            send_sem=dual_send_sem.at[0, 0, 0],
            recv_sem=dual_recv_sem.at[0, 0, c],
            device_id={"bus": sibling},
            device_id_type=MESH,
        )

    def send_flow(t, k, part):
        return pltpu.make_async_remote_copy(
            src_ref=flow_send.at[t, peer(k), rows(part)],
            dst_ref=flow_recv.at[t, chip, rows(part)],
            send_sem=flow_send_sem.at[t, part, k],
            recv_sem=flow_recv_sem.at[t, part, chip],
            device_id={"bus": 2 * peer(k) + core},
            device_id_type=MESH,
        )

    def recv_flow(t, c, part):
        return pltpu.make_async_remote_copy(
            src_ref=flow_recv.at[t, c, rows(part)],
            dst_ref=flow_recv.at[t, c, rows(part)],
            send_sem=flow_send_sem.at[t, part, 0],
            recv_sem=flow_recv_sem.at[t, part, c],
            device_id={"bus": sibling},
            device_id_type=MESH,
        )

    def to_sibling(source, target, sems):
        return pltpu.make_async_remote_copy(
            src_ref=source,
            dst_ref=target,
            send_sem=sems.at[0],
            recv_sem=sems.at[1],
            device_id={"bus": sibling},
            device_id_type=MESH,
        )

    for fetch in fetches[:3]:
        fetch.wait()
    pack_index = jnp.full((8, LANES), -1, jnp.int32)
    lane8 = lax.broadcasted_iota(jnp.int32, (8, LANES), 1)
    for at, ref in ((0, gen_bus_ref), (units, stor_bus_ref)):
        padded = jnp.concatenate([ref[...], jnp.zeros((1, LANES - units), jnp.int32)], axis=1)
        padded = pltpu.roll(jnp.broadcast_to(padded, (8, LANES)), at, 1)
        pack_index = jnp.where((lane8 >= at) & (lane8 < at + units), padded - me * buses, pack_index)
    bus_id = lax.broadcasted_iota(jnp.int32, (buses, LANES), 0)
    onehot = jnp.where(bus_id == pack_index[0:1, :], 1.0, 0.0)
    loads = jnp.concatenate(
        [
            jnp.zeros((half, buses), jnp.float32),
            load_ref[...].astype(jnp.float32),
            jnp.zeros((LANES - half - hours, buses), jnp.float32),
        ],
        axis=0,
    )
    place = onehot + loads.T
    place_buf[0] = place.astype(jnp.bfloat16)
    place_buf[1] = pltpu.roll(place, half, 1).astype(jnp.bfloat16)

    for fetch in fetches[3:]:
        fetch.wait()
    gens = slice(0, units)
    stors = slice(units, half)
    pack_own[...] = jnp.zeros_like(pack_own)
    pack_own[0, :, gens] = gen_ref[...]
    pack_own[0, :, stors] = charge_ref[...]
    pack_own[1, :, stors] = energy_ref[...]
    pack_own[2, 0:1, gens] = cost_ref[...]
    pack_own[2, 1:2, gens] = gen_max_ref[...]
    first = me * units
    lane_start = pl.multiple_of(lax.div(first, LANES) * LANES, LANES)
    shift = lax.rem(units - lax.rem(first, LANES) + LANES, LANES)
    for row, ref in ((1, charge_max_ref), (2, init_ref), (3, energy_max_ref)):
        chunk = jnp.broadcast_to(ref[0:1, pl.ds(lane_start, LANES)], (8, LANES))
        pack_own[2, row : row + 1, stors] = pltpu.roll(chunk, shift, 1)[0:1, stors]

    pl.semaphore_wait(barrier, chips)
    dual_in.wait()
    for k in far_first:
        send_first(k).start()
    send_pack = to_sibling(pack_own, pack_sib, pack_sem)
    send_pack.start()

    together = 2 if chips % 2 == 0 else 1
    taking = together * block

    def take_columns(slot, placed):
        high, low = split_bf16(factors_buf[pl.ds(slot, together)].reshape(taking, buses))
        taken = jnp.dot(
            jnp.concatenate([high, low], axis=0),
            place_buf[placed],
            preferred_element_type=jnp.float32,
        )
        return taken[:taking] + taken[taking:]

    def swap_columns(i):
        return pltpu.make_async_remote_copy(
            src_ref=cols_send.at[i],
            dst_ref=cols_recv.at[i],
            send_sem=cols_sems.at[0, i],
            recv_sem=cols_sems.at[1, i],
            device_id={"bus": sibling},
            device_id_type=MESH,
        )

    @pl.loop(0, chips // together)
    def _(step):
        turns = [step * together + j for j in range(together)]
        for i in turns:
            load_factors(i).wait()
        taken = take_columns(step * together, 1)
        for j, i in enumerate(turns):
            cols_send[i] = taken[j * block : (j + 1) * block]
            swap_columns(i).start()

    for k in reversed(far_first):
        recv_first(peer(chips - k)).wait_recv()

    def collect(step, total):
        turns = [step * together + j for j in range(together)]
        for i in turns:
            load_factors(chips + i).wait()
        for i in turns:
            swap_columns(i).wait()
        taken = take_columns(chips + step * together, 0)
        for j, i in enumerate(turns):
            mine = taken[j * block : (j + 1) * block]
            other = cols_recv[i]
            lane_at = lax.broadcasted_iota(jnp.int32, mine.shape, 1)
            columns = jnp.where(lane_at < half, mine, other)
            turned = jnp.concatenate(split_bf16(columns), axis=1)
            turned_buf[i] = turned
            high, low = split_bf16(columns.T)
            lines_at = pl.ds(pl.multiple_of(i * block, block), block)
            weight_buf[0:width, lines_at] = high
            weight_buf[width : 2 * width, lines_at] = low
            demand = mine + pltpu.roll(other, half, 1)
            demand_buf[i] = load_unit * demand.T[half : half + hours]
            pieces = jnp.concatenate(split_bf16(dual_buf[0, i]), axis=0)
            total = total + jnp.dot(pieces, turned, preferred_element_type=jnp.float32)
        return total

    total = lax.fori_loop(
        0, chips // together, collect, jnp.zeros((2 * hours, 2 * width), jnp.float32)
    )
    total = total[:hours] + total[hours:]
    total = total[:, :width] + total[:, width:]

    send_pack.wait()
    state = pack_own[0] + pltpu.roll(pack_sib[0], half, 1)
    energy_dual = pack_own[1] + pltpu.roll(pack_sib[1], half, 1)
    params = pack_own[2] + pltpu.roll(pack_sib[2], half, 1)
    cost, upper, start_energy, energy_limit = (params[r : r + 1] for r in range(4))
    lane = lax.broadcasted_iota(jnp.int32, (hours, width), 1)
    is_gen = lax.rem(lane, half) < units
    lower = jnp.where(is_gen, 0.0, -upper)
    later = running_sum(energy_dual, True)
    own_dual = [dual_buf[0, chip, rows(part)] for part in range(PARTS)]
    state = [state[rows(part)] for part in range(PARTS)]
    is_gen_part, lower_part = is_gen[:part_rows], lower[:part_rows]
    line_max = line_max_ref[...]

    def stacked(values):
        high = values.astype(jnp.bfloat16).astype(jnp.float32)
        return jnp.concatenate([high, values - high], axis=0).astype(jnp.bfloat16)

    def swap_prices(t, part):
        return to_sibling(
            price_send.at[t, rows(part)], price_recv.at[t, rows(part)], price_sem.at[t, part]
        )

    def partial_prices(t, part):
        for k in far_first[::-1]:
            recv_dual(t, peer(chips - k), part).wait_recv()
        duals = jnp.concatenate([dual_buf[t, c, rows(part)] for c in range(chips)], axis=1)
        turned = turned_buf[...].reshape(chips * block, 2 * width)
        total = jnp.dot(stacked(duals), turned, preferred_element_type=jnp.float32)
        total = total[:part_rows] + total[part_rows:]
        return total[:, :width] + total[:, width:]

    def offer_prices(t, part, partial):
        price_send[t, rows(part)] = partial
        swap_prices(t, part).start()

    def iterate(t, carry, last):
        state, energy_dual, later, own_dual, partial = carry
        new_state, bars, line_flows = [], [], []
        for part in range(PARTS):
            swap_prices(t, part).wait()
            prices = partial[part] + pltpu.roll(price_recv[t, rows(part)], half, 1)
            pull = efficiency * interval * later[rows(part)]
            gradient = jnp.where(is_gen_part, cost + prices, pull - prices)
            step = jnp.clip(state[part] - primal_step * gradient, lower_part, upper)
            bar = 2.0 * step - state[part]
            new_state.append(step)
            bars.append(bar)
            pieces = stacked(jnp.where(is_gen_part, bar, -bar))
            pieces = jnp.concatenate([pieces, pieces], axis=1)

            out = jnp.dot(pieces, weight_buf[...], preferred_element_type=jnp.float32)
            out = out[:part_rows] + out[part_rows:]
            for c in range(chips):
                flow = out[:, c * block : (c + 1) * block] - demand_buf[c, rows(part)]
                flow_send[t, c, rows(part)] = flow
            for k in far_first:
                send_flow(t, k, part).start()
            line_flows.append(flow_send[t, chip, rows(part)])

        if last:
            for part in range(PARTS):
                gen_out[rows(part)] = new_state[part][:, gens]
                charge_out[rows(part)] = new_state[part][:, stors]
            stores[0].start()
            stores[1].start()
        so_far = running_sum(jnp.concatenate(bars, axis=0), False)
        energy = start_energy + efficiency * interval * so_far
        energy_dual = clip_dual(energy_dual + energy_step * energy, energy_step, 0.0, energy_limit)
        if last:
            energy_out[...] = energy_dual[:, stors]
            stores[2].start()
        else:
            later = running_sum(energy_dual, True)

        new_dual, new_partial = [], []
        for part in range(PARTS):
            flow = line_flows[part]
            for k in far_first[::-1]:
                c = peer(chips - k)
                recv_flow(t, c, part).wait_recv()
                flow = flow + flow_recv[t, c, rows(part)]
            dual = clip_dual(own_dual[part] + dual_step * flow, dual_step, -line_max, line_max)
            new_dual.append(dual)
            if last:
                dual_out[rows(part)] = dual
            else:
                dual_buf[t + 1, chip, rows(part)] = dual
                for k in far_first:
                    send_dual(t + 1, k, part).start()
        if last:
            stores[3].start()
        else:
            for part in range(PARTS):
                new_partial.append(partial_prices(t + 1, part))
                offer_prices(t + 1, part, new_partial[part])
        return new_state, energy_dual, later, new_dual, new_partial

    partial = [total[rows(part)] for part in range(PARTS)]
    for part in range(PARTS):
        offer_prices(0, part, partial[part])
    carry = (state, energy_dual, later, own_dual, partial)
    carry = lax.fori_loop(0, ITERS - 1, lambda t, carry: iterate(t, carry, False), carry)
    iterate(ITERS - 1, carry, True)

    for k in range(1, chips):
        send_first(k).wait_send()

    @pl.loop(0, ITERS)
    def _(t):
        for part in range(PARTS):
            for k in range(1, chips):
                send_flow(t, k, part).wait_send()

    @pl.loop(1, ITERS)
    def _(t):
        for part in range(PARTS):
            for k in range(1, chips):
                send_dual(t, k, part).wait_send()

    for store in stores:
        store.wait()


def store_kernel(*refs):
    count = len(refs) // 3
    sems = refs[-1]
    fetches = [
        pltpu.make_async_copy(refs[at], refs[2 * count + at], sems.at[0, at]) for at in range(count)
    ]
    stores = [
        pltpu.make_async_copy(refs[2 * count + at], refs[count + at], sems.at[1, at])
        for at in range(count)
    ]
    for fetch in fetches:
        fetch.start()
    for fetch, store in zip(fetches, stores):
        fetch.wait()
        store.start()
    for store in stores:
        store.wait()


def on_device_kernel(
    generation,
    charging,
    flow_dual,
    energy_dual,
    shift_factors,
    load_units,
    generator_bus,
    storage_bus,
    generator_cost,
    generator_max,
    charging_max,
    energy_init,
    energy_max,
    line_max,
):
    lines, buses = shift_factors.shape
    units, hours = generation.shape
    block = flow_dual.shape[0]
    n_bus = lines // block
    chips = n_bus // 2
    half = 2 * units
    width = 2 * half
    hbm = pl.BlockSpec(memory_space=pltpu.HBM)
    f32 = jnp.float32
    dma = pltpu.SemaphoreType.DMA
    arrays = (
        generation.T,
        charging,
        flow_dual.T,
        energy_dual,
        shift_factors,
        load_units.T,
        generator_bus[None, :],
        storage_bus[None, :],
        generator_cost[None, :],
        generator_max[None, :],
        charging_max[None, :],
        energy_init[None, :],
        energy_max[None, :],
        line_max[None, :],
    )
    out_shape = (
        jax.ShapeDtypeStruct((hours, units), f32),
        jax.ShapeDtypeStruct((hours, units), f32),
        jax.ShapeDtypeStruct((hours, block), f32),
        jax.ShapeDtypeStruct((hours, units), f32),
    )
    results = pl.pallas_call(
        functools.partial(iterate_kernel, n_bus),
        out_shape=out_shape,
        in_specs=[hbm] * len(arrays),
        out_specs=(hbm,) * 4,
        scratch_shapes=[
            pltpu.VMEM(array.shape, array.dtype)
            for at, array in enumerate(arrays)
            if at not in (2, 4)
        ]
        + [pltpu.VMEM(result.shape, f32) for result in out_shape]
        + [
            pltpu.VMEM((n_bus, block, buses), f32),
            pltpu.VMEM((2, buses, LANES), jnp.bfloat16),
            pltpu.VMEM((3, hours, width), f32),
            pltpu.VMEM((3, hours, width), f32),
            pltpu.VMEM((chips, block, LANES), f32),
            pltpu.VMEM((chips, block, LANES), f32),
            pltpu.VMEM((2 * width, chips * block), jnp.bfloat16),
            pltpu.VMEM((chips, block, 2 * width), jnp.bfloat16),
            pltpu.VMEM((chips, hours, block), f32),
            pltpu.VMEM((ITERS, chips, hours, block), f32),
            pltpu.VMEM((ITERS, chips, hours, block), f32),
            pltpu.VMEM((ITERS, chips, hours, block), f32),
            pltpu.VMEM((ITERS, hours, width), f32),
            pltpu.VMEM((ITERS, hours, width), f32),
            dma((len(arrays) - 1,)),
            dma((4,)),
            dma((n_bus,)),
            dma((2,)),
            dma((2, chips)),
            dma((ITERS, PARTS, chips)),
            dma((ITERS, PARTS, chips)),
            dma((ITERS, PARTS, chips)),
            dma((ITERS, PARTS, chips)),
            dma((ITERS, PARTS, 2)),
        ],
        compiler_params=pltpu.CompilerParams(
            collective_id=0, has_side_effects=True, vmem_limit_bytes=VMEM_BYTES
        ),
    )(*arrays)
    gen_new, charge_new, dual_new, energy_new = pl.pallas_call(
        store_kernel,
        out_shape=out_shape,
        in_specs=[hbm] * 4,
        out_specs=(hbm,) * 4,
        scratch_shapes=[pltpu.VMEM(result.shape, f32) for result in out_shape] + [dma((2, 4))],
        compiler_params=pltpu.CompilerParams(vmem_limit_bytes=VMEM_BYTES),
    )(*results)
    return gen_new.T, charge_new, dual_new.T, energy_new


def on_device(
    generation,
    charging,
    flow_dual,
    energy_dual,
    shift_factors,
    load_units,
    generator_bus,
    storage_bus,
    generator_cost,
    generator_max,
    charging_max,
    energy_init,
    energy_max,
    line_max,
):
    bus_local = shift_factors.shape[1]
    gen_local = generator_bus.shape[0]
    stor_local = storage_bus.shape[0]
    own_index = lax.axis_index("bus")
    bus_ids = lax.broadcasted_iota(jnp.int32, (bus_local, 1), 0) + own_index * bus_local
    gen_onehot = (generator_bus[None, :] == bus_ids).astype(jnp.float32)
    stor_onehot = (storage_bus[None, :] == bus_ids).astype(jnp.float32)
    columns = contract(shift_factors, jnp.concatenate([gen_onehot, stor_onehot], axis=1), inner_pair)
    demand = load_units.astype(jnp.float32) * load_unit
    demand_flows = contract(shift_factors, demand, inner_pair)
    unit_cost = generator_cost[:, None]
    ceiling = generator_max[:, None]
    first_slot = own_index * stor_local
    charge_limit = lax.dynamic_slice_in_dim(charging_max, first_slot, stor_local)[None, :]
    start_energy = lax.dynamic_slice_in_dim(energy_init, first_slot, stor_local)[None, :]
    energy_limit = lax.dynamic_slice_in_dim(energy_max, first_slot, stor_local)[None, :]
    for iteration in range(ITERS):
        prices = contract(columns, lax.all_gather(flow_dual, "bus", axis=0, tiled=True), across_first)
        gen_step = jnp.clip(
            generation - primal_step * (unit_cost + prices[:gen_local]), 0.0, ceiling
        )
        gen_bar = 2.0 * gen_step - generation
        stor_prices = prices[gen_local:].T
        gradient = efficiency * interval * reverse_cumsum(energy_dual) - stor_prices
        charge_step = jnp.clip(charging - primal_step * gradient, -charge_limit, charge_limit)
        bar_bus = 2.0 * charge_step - charging
        energy = start_energy + efficiency * interval * jnp.cumsum(bar_bus, axis=0)
        energy_dual = clip_dual(energy_dual + energy_step * energy, energy_step, 0.0, energy_limit)
        charging = charge_step
        bars = jnp.concatenate([gen_bar, -bar_bus.T], axis=0)
        line_flows = lax.psum_scatter(
            contract(columns, bars, inner_pair) - demand_flows, "bus", scatter_dimension=0, tiled=True
        )
        flow_dual = clip_dual(
            flow_dual + dual_step * line_flows, dual_step, -line_max[:, None], line_max[:, None]
        )
        generation = gen_step
    return (generation, charging, flow_dual, energy_dual)


def fits_kernel(n_bus, generation, charging, flow_dual, shift_factors, storage_bus):
    units = generation.shape[0] // n_bus
    stors = storage_bus.shape[0] // n_bus
    block = flow_dual.shape[0] // n_bus
    hours = charging.shape[0] // 2
    buses = shift_factors.shape[1] // n_bus
    return (
        n_bus % 2 == 0
        and units == stors
        and 4 * units == LANES
        and hours == 16
        and block % LANES == 0
        and buses % LANES == 0
        and shift_factors.shape[0] * buses * 4 <= 2**24
    )


def solution(mesh):
    placed = (
        P("bus", "groups"),
        P("groups", "bus"),
        P("bus", "groups"),
        P("groups", "bus"),
        P(None, "bus"),
        P("bus", "groups"),
        P("bus"),
        P("bus"),
        P("bus"),
        P("bus"),
        P(),
        P(),
        P(),
        P("bus"),
    )
    n_bus = mesh.shape["bus"]

    def whole(*arrays):
        fits = mesh.shape["groups"] == 2 and fits_kernel(
            n_bus, arrays[0], arrays[1], arrays[2], arrays[4], arrays[7]
        )
        return jax.shard_map(
            on_device_kernel if fits else on_device,
            mesh=mesh,
            in_specs=placed,
            out_specs=(P("bus", "groups"), P("groups", "bus"), P("bus", "groups"), P("groups", "bus")),
            check_vma=False,
        )(*arrays)

    return whole
```

```python
import functools

import jax
import jax.numpy as jnp
from jax import lax
from jax.experimental import pallas as pl
from jax.experimental.pallas import tpu as pltpu
from jax.sharding import PartitionSpec as P

ITERS = 3
LANES = 128
PARTS = 1
VMEM_BYTES = 65472 * 1024
MESH = pl.DeviceIdType.MESH

primal_step = 0.5
dual_step = 0.5
energy_step = 0.05
efficiency = 0.95
interval = 0.125
load_unit = 0.05
highest = lax.Precision.HIGHEST
across_first = (((0,), (0,)), ((), ()))
across_second = (((1,), (1,)), ((), ()))
inner_pair = (((1,), (0,)), ((), ()))


def contract(left, right, dims):
    return lax.dot_general(left, right, dims, precision=highest, preferred_element_type=jnp.float32)


def reverse_cumsum(values):
    return jnp.flip(jnp.cumsum(jnp.flip(values, 0), axis=0), 0)


def clip_dual(shifted, step_size, low_bound, high_bound):
    return shifted - step_size * jnp.clip(shifted / step_size, low_bound, high_bound)


def split_bf16(values):
    high = values.astype(jnp.bfloat16)
    return high, (values - high.astype(jnp.float32)).astype(jnp.bfloat16)


def running_sum(values, backward):
    rows = values.shape[0]
    row = lax.broadcasted_iota(jnp.int32, values.shape, 0)
    step = 1
    while step < rows:
        if backward:
            moved = jnp.where(row < rows - step, pltpu.roll(values, rows - step, 0), 0.0)
        else:
            moved = jnp.where(row >= step, pltpu.roll(values, step, 0), 0.0)
        values = values + moved
        step *= 2
    return values


def iterate_kernel(
    n_bus,
    gen_hbm,
    charge_hbm,
    dual_hbm,
    energy_hbm,
    factors_hbm,
    load_hbm,
    gen_bus_hbm,
    stor_bus_hbm,
    cost_hbm,
    gen_max_hbm,
    charge_max_hbm,
    init_hbm,
    energy_max_hbm,
    line_max_hbm,
    gen_hbm_out,
    charge_hbm_out,
    dual_hbm_out,
    energy_hbm_out,
    gen_ref,
    charge_ref,
    energy_ref,
    load_ref,
    gen_bus_ref,
    stor_bus_ref,
    cost_ref,
    gen_max_ref,
    charge_max_ref,
    init_ref,
    energy_max_ref,
    line_max_ref,
    gen_out,
    charge_out,
    dual_out,
    energy_out,
    factors_buf,
    place_buf,
    pack_own,
    pack_sib,
    cols_send,
    cols_recv,
    weight_buf,
    turned_buf,
    demand_buf,
    dual_buf,
    flow_send,
    flow_recv,
    price_send,
    price_recv,
    input_sem,
    output_sem,
    factors_sem,
    pack_sem,
    cols_sems,
    dual_send_sem,
    dual_recv_sem,
    flow_send_sem,
    flow_recv_sem,
    price_sem,
):
    chips = n_bus // 2
    hours, units = gen_ref.shape
    block = dual_hbm.shape[1]
    buses = factors_hbm.shape[1]
    half = 2 * units
    width = 2 * half
    me = lax.axis_index("bus")
    core = lax.rem(me, 2)
    chip = lax.div(me, 2)
    sibling = me + 1 - 2 * core
    far_first = sorted(range(1, chips), key=lambda k: abs(2 * k - chips))

    def peer(k):
        return lax.rem(chip + k, chips)

    barrier = pltpu.get_barrier_semaphore()
    for k in range(1, chips):
        pl.semaphore_signal(
            barrier, inc=1, device_id={"bus": 2 * peer(k) + core}, device_id_type=MESH
        )
    pl.semaphore_signal(barrier, inc=1, device_id={"bus": sibling}, device_id_type=MESH)

    dual_in = pltpu.make_async_copy(dual_hbm, dual_buf.at[0, chip], input_sem.at[0])
    fetches = [
        pltpu.make_async_copy(source, target, input_sem.at[1 + at])
        for at, (source, target) in enumerate(
            (
                (load_hbm, load_ref),
                (gen_bus_hbm, gen_bus_ref),
                (stor_bus_hbm, stor_bus_ref),
                (gen_hbm, gen_ref),
                (charge_hbm, charge_ref),
                (energy_hbm, energy_ref),
                (cost_hbm, cost_ref),
                (gen_max_hbm, gen_max_ref),
                (charge_max_hbm, charge_max_ref),
                (init_hbm, init_ref),
                (energy_max_hbm, energy_max_ref),
                (line_max_hbm, line_max_ref),
            )
        )
    ]
    stores = [
        pltpu.make_async_copy(source, target, output_sem.at[at])
        for at, (source, target) in enumerate(
            (
                (gen_out, gen_hbm_out),
                (charge_out, charge_hbm_out),
                (energy_out, energy_hbm_out),
                (dual_out, dual_hbm_out),
            )
        )
    ]
    dual_in.start()
    for fetch in fetches:
        fetch.start()

    def load_factors(slot):
        own = lax.div(slot, chips)
        b = 2 * lax.rem(slot, chips) + lax.rem(core + 1 + own, 2)
        start = pl.multiple_of(b * block, block)
        return pltpu.make_async_copy(
            factors_hbm.at[pl.ds(start, block), :], factors_buf.at[slot], factors_sem.at[slot]
        )

    @pl.loop(0, n_bus)
    def _(slot):
        load_factors(slot).start()

    part_rows = hours // PARTS

    def rows(part):
        return slice(part * part_rows, (part + 1) * part_rows)

    def send_dual(t, k, part):
        return pltpu.make_async_remote_copy(
            src_ref=dual_buf.at[t, chip, rows(part)],
            dst_ref=dual_buf.at[t, chip, rows(part)],
            send_sem=dual_send_sem.at[t, part, k],
            recv_sem=dual_recv_sem.at[t, part, chip],
            device_id={"bus": 2 * peer(k) + core},
            device_id_type=MESH,
        )

    def recv_dual(t, c, part):
        return pltpu.make_async_remote_copy(
            src_ref=dual_buf.at[t, c, rows(part)],
            dst_ref=dual_buf.at[t, c, rows(part)],
            send_sem=dual_send_sem.at[t, part, 0],
            recv_sem=dual_recv_sem.at[t, part, c],
            device_id={"bus": sibling},
            device_id_type=MESH,
        )

    def send_first(k):
        return pltpu.make_async_remote_copy(
            src_ref=dual_buf.at[0, chip],
            dst_ref=dual_buf.at[0, chip],
            send_sem=dual_send_sem.at[0, 0, k],
            recv_sem=dual_recv_sem.at[0, 0, chip],
            device_id={"bus": 2 * peer(k) + core},
            device_id_type=MESH,
        )

    def recv_first(c):
        return pltpu.make_async_remote_copy(
            src_ref=dual_buf.at[0, c],
            dst_ref=dual_buf.at[0, c],
            send_sem=dual_send_sem.at[0, 0, 0],
            recv_sem=dual_recv_sem.at[0, 0, c],
            device_id={"bus": sibling},
            device_id_type=MESH,
        )

    def send_flow(t, k, part):
        return pltpu.make_async_remote_copy(
            src_ref=flow_send.at[t, peer(k), rows(part)],
            dst_ref=flow_recv.at[t, chip, rows(part)],
            send_sem=flow_send_sem.at[t, part, k],
            recv_sem=flow_recv_sem.at[t, part, chip],
            device_id={"bus": 2 * peer(k) + core},
            device_id_type=MESH,
        )

    def recv_flow(t, c, part):
        return pltpu.make_async_remote_copy(
            src_ref=flow_recv.at[t, c, rows(part)],
            dst_ref=flow_recv.at[t, c, rows(part)],
            send_sem=flow_send_sem.at[t, part, 0],
            recv_sem=flow_recv_sem.at[t, part, c],
            device_id={"bus": sibling},
            device_id_type=MESH,
        )

    def to_sibling(source, target, sems):
        return pltpu.make_async_remote_copy(
            src_ref=source,
            dst_ref=target,
            send_sem=sems.at[0],
            recv_sem=sems.at[1],
            device_id={"bus": sibling},
            device_id_type=MESH,
        )

    for fetch in fetches[:3]:
        fetch.wait()
    pack_index = jnp.full((8, LANES), -1, jnp.int32)
    lane8 = lax.broadcasted_iota(jnp.int32, (8, LANES), 1)
    for at, ref in ((0, gen_bus_ref), (units, stor_bus_ref)):
        padded = jnp.concatenate([ref[...], jnp.zeros((1, LANES - units), jnp.int32)], axis=1)
        padded = pltpu.roll(jnp.broadcast_to(padded, (8, LANES)), at, 1)
        pack_index = jnp.where((lane8 >= at) & (lane8 < at + units), padded - me * buses, pack_index)
    bus_id = lax.broadcasted_iota(jnp.int32, (buses, LANES), 0)
    onehot = jnp.where(bus_id == pack_index[0:1, :], 1.0, 0.0)
    loads = jnp.concatenate(
        [
            jnp.zeros((half, buses), jnp.float32),
            load_ref[...].astype(jnp.float32),
            jnp.zeros((LANES - half - hours, buses), jnp.float32),
        ],
        axis=0,
    )
    place = onehot + loads.T
    place_buf[0] = place.astype(jnp.bfloat16)
    place_buf[1] = pltpu.roll(place, half, 1).astype(jnp.bfloat16)

    for fetch in fetches[3:]:
        fetch.wait()
    gens = slice(0, units)
    stors = slice(units, half)
    pack_own[...] = jnp.zeros_like(pack_own)
    pack_own[0, :, gens] = gen_ref[...]
    pack_own[0, :, stors] = charge_ref[...]
    pack_own[1, :, stors] = energy_ref[...]
    pack_own[2, 0:1, gens] = cost_ref[...]
    pack_own[2, 1:2, gens] = gen_max_ref[...]
    first = me * units
    lane_start = pl.multiple_of(lax.div(first, LANES) * LANES, LANES)
    shift = lax.rem(units - lax.rem(first, LANES) + LANES, LANES)
    for row, ref in ((1, charge_max_ref), (2, init_ref), (3, energy_max_ref)):
        chunk = jnp.broadcast_to(ref[0:1, pl.ds(lane_start, LANES)], (8, LANES))
        pack_own[2, row : row + 1, stors] = pltpu.roll(chunk, shift, 1)[0:1, stors]

    pl.semaphore_wait(barrier, chips)
    dual_in.wait()
    for k in far_first:
        send_first(k).start()
    send_pack = to_sibling(pack_own, pack_sib, pack_sem)
    send_pack.start()

    together = 2 if chips % 2 == 0 else 1
    taking = together * block

    def take_columns(slot, placed):
        high, low = split_bf16(factors_buf[pl.ds(slot, together)].reshape(taking, buses))
        taken = jnp.dot(
            jnp.concatenate([high, low], axis=0),
            place_buf[placed],
            preferred_element_type=jnp.float32,
        )
        return taken[:taking] + taken[taking:]

    def swap_columns(i):
        return pltpu.make_async_remote_copy(
            src_ref=cols_send.at[i],
            dst_ref=cols_recv.at[i],
            send_sem=cols_sems.at[0, i],
            recv_sem=cols_sems.at[1, i],
            device_id={"bus": sibling},
            device_id_type=MESH,
        )

    @pl.loop(0, chips // together)
    def _(step):
        turns = [step * together + j for j in range(together)]
        for i in turns:
            load_factors(i).wait()
        taken = take_columns(step * together, 1)
        for j, i in enumerate(turns):
            cols_send[i] = taken[j * block : (j + 1) * block]
            swap_columns(i).start()

    for k in reversed(far_first):
        recv_first(peer(chips - k)).wait_recv()

    def collect(step, total):
        turns = [step * together + j for j in range(together)]
        for i in turns:
            load_factors(chips + i).wait()
        for i in turns:
            swap_columns(i).wait()
        taken = take_columns(chips + step * together, 0)
        for j, i in enumerate(turns):
            mine = taken[j * block : (j + 1) * block]
            other = cols_recv[i]
            lane_at = lax.broadcasted_iota(jnp.int32, mine.shape, 1)
            columns = jnp.where(lane_at < half, mine, other)
            turned = jnp.concatenate(split_bf16(columns), axis=1)
            turned_buf[i] = turned
            high, low = split_bf16(columns.T)
            lines_at = pl.ds(pl.multiple_of(i * block, block), block)
            weight_buf[0:width, lines_at] = high
            weight_buf[width : 2 * width, lines_at] = low
            demand = mine + pltpu.roll(other, half, 1)
            demand_buf[i] = load_unit * demand.T[half : half + hours]
            pieces = jnp.concatenate(split_bf16(dual_buf[0, i]), axis=0)
            total = total + jnp.dot(pieces, turned, preferred_element_type=jnp.float32)
        return total

    total = lax.fori_loop(
        0, chips // together, collect, jnp.zeros((2 * hours, 2 * width), jnp.float32)
    )
    total = total[:hours] + total[hours:]
    total = total[:, :width] + total[:, width:]

    send_pack.wait()
    state = pack_own[0] + pltpu.roll(pack_sib[0], half, 1)
    energy_dual = pack_own[1] + pltpu.roll(pack_sib[1], half, 1)
    params = pack_own[2] + pltpu.roll(pack_sib[2], half, 1)
    cost, upper, start_energy, energy_limit = (params[r : r + 1] for r in range(4))
    lane = lax.broadcasted_iota(jnp.int32, (hours, width), 1)
    is_gen = lax.rem(lane, half) < units
    lower = jnp.where(is_gen, 0.0, -upper)
    later = running_sum(energy_dual, True)
    own_dual = [dual_buf[0, chip, rows(part)] for part in range(PARTS)]
    state = [state[rows(part)] for part in range(PARTS)]
    is_gen_part, lower_part = is_gen[:part_rows], lower[:part_rows]
    line_max = line_max_ref[...]

    def stacked(values):
        high = values.astype(jnp.bfloat16).astype(jnp.float32)
        return jnp.concatenate([high, values - high], axis=0).astype(jnp.bfloat16)

    def swap_prices(t, part):
        return to_sibling(
            price_send.at[t, rows(part)], price_recv.at[t, rows(part)], price_sem.at[t, part]
        )

    def partial_prices(t, part):
        for k in far_first[::-1]:
            recv_dual(t, peer(chips - k), part).wait_recv()
        duals = jnp.concatenate([dual_buf[t, c, rows(part)] for c in range(chips)], axis=1)
        turned = turned_buf[...].reshape(chips * block, 2 * width)
        total = jnp.dot(stacked(duals), turned, preferred_element_type=jnp.float32)
        total = total[:part_rows] + total[part_rows:]
        return total[:, :width] + total[:, width:]

    def offer_prices(t, part, partial):
        price_send[t, rows(part)] = partial
        swap_prices(t, part).start()

    def iterate(t, carry, last):
        state, energy_dual, later, own_dual, partial = carry
        new_state, bars, line_flows = [], [], []
        for part in range(PARTS):
            swap_prices(t, part).wait()
            prices = partial[part] + pltpu.roll(price_recv[t, rows(part)], half, 1)
            pull = efficiency * interval * later[rows(part)]
            gradient = jnp.where(is_gen_part, cost + prices, pull - prices)
            step = jnp.clip(state[part] - primal_step * gradient, lower_part, upper)
            bar = 2.0 * step - state[part]
            new_state.append(step)
            bars.append(bar)
            pieces = stacked(jnp.where(is_gen_part, bar, -bar))
            pieces = jnp.concatenate([pieces, pieces], axis=1)

            out = jnp.dot(pieces, weight_buf[...], preferred_element_type=jnp.float32)
            out = out[:part_rows] + out[part_rows:]
            for c in range(chips):
                flow = out[:, c * block : (c + 1) * block] - demand_buf[c, rows(part)]
                flow_send[t, c, rows(part)] = flow
            for k in far_first:
                send_flow(t, k, part).start()
            line_flows.append(flow_send[t, chip, rows(part)])

        if last:
            for part in range(PARTS):
                gen_out[rows(part)] = new_state[part][:, gens]
                charge_out[rows(part)] = new_state[part][:, stors]
            stores[0].start()
            stores[1].start()
        so_far = running_sum(jnp.concatenate(bars, axis=0), False)
        energy = start_energy + efficiency * interval * so_far
        energy_dual = clip_dual(energy_dual + energy_step * energy, energy_step, 0.0, energy_limit)
        if last:
            energy_out[...] = energy_dual[:, stors]
            stores[2].start()
        else:
            later = running_sum(energy_dual, True)

        new_dual, new_partial = [], []
        for part in range(PARTS):
            flow = line_flows[part]
            for k in far_first[::-1]:
                c = peer(chips - k)
                recv_flow(t, c, part).wait_recv()
                flow = flow + flow_recv[t, c, rows(part)]
            dual = clip_dual(own_dual[part] + dual_step * flow, dual_step, -line_max, line_max)
            new_dual.append(dual)
            if last:
                dual_out[rows(part)] = dual
            else:
                dual_buf[t + 1, chip, rows(part)] = dual
                for k in far_first:
                    send_dual(t + 1, k, part).start()
        if last:
            stores[3].start()
        else:
            for part in range(PARTS):
                new_partial.append(partial_prices(t + 1, part))
                offer_prices(t + 1, part, new_partial[part])
        return new_state, energy_dual, later, new_dual, new_partial

    partial = [total[rows(part)] for part in range(PARTS)]
    for part in range(PARTS):
        offer_prices(0, part, partial[part])
    carry = (state, energy_dual, later, own_dual, partial)
    carry = lax.fori_loop(0, ITERS - 1, lambda t, carry: iterate(t, carry, False), carry)
    iterate(ITERS - 1, carry, True)

    for k in range(1, chips):
        send_first(k).wait_send()

    @pl.loop(0, ITERS)
    def _(t):
        for part in range(PARTS):
            for k in range(1, chips):
                send_flow(t, k, part).wait_send()

    @pl.loop(1, ITERS)
    def _(t):
        for part in range(PARTS):
            for k in range(1, chips):
                send_dual(t, k, part).wait_send()

    for store in stores:
        store.wait()


def store_kernel(*refs):
    count = len(refs) // 3
    sems = refs[-1]
    fetches = [
        pltpu.make_async_copy(refs[at], refs[2 * count + at], sems.at[0, at]) for at in range(count)
    ]
    stores = [
        pltpu.make_async_copy(refs[2 * count + at], refs[count + at], sems.at[1, at])
        for at in range(count)
    ]
    for fetch in fetches:
        fetch.start()
    for fetch, store in zip(fetches, stores):
        fetch.wait()
        store.start()
    for store in stores:
        store.wait()


def on_device_kernel(
    generation,
    charging,
    flow_dual,
    energy_dual,
    shift_factors,
    load_units,
    generator_bus,
    storage_bus,
    generator_cost,
    generator_max,
    charging_max,
    energy_init,
    energy_max,
    line_max,
):
    lines, buses = shift_factors.shape
    units, hours = generation.shape
    block = flow_dual.shape[0]
    n_bus = lines // block
    chips = n_bus // 2
    half = 2 * units
    width = 2 * half
    hbm = pl.BlockSpec(memory_space=pltpu.HBM)
    f32 = jnp.float32
    dma = pltpu.SemaphoreType.DMA
    arrays = (
        generation.T,
        charging,
        flow_dual.T,
        energy_dual,
        shift_factors,
        load_units.T,
        generator_bus[None, :],
        storage_bus[None, :],
        generator_cost[None, :],
        generator_max[None, :],
        charging_max[None, :],
        energy_init[None, :],
        energy_max[None, :],
        line_max[None, :],
    )
    out_shape = (
        jax.ShapeDtypeStruct((hours, units), f32),
        jax.ShapeDtypeStruct((hours, units), f32),
        jax.ShapeDtypeStruct((hours, block), f32),
        jax.ShapeDtypeStruct((hours, units), f32),
    )
    results = pl.pallas_call(
        functools.partial(iterate_kernel, n_bus),
        out_shape=out_shape,
        in_specs=[hbm] * len(arrays),
        out_specs=(hbm,) * 4,
        scratch_shapes=[
            pltpu.VMEM(array.shape, array.dtype)
            for at, array in enumerate(arrays)
            if at not in (2, 4)
        ]
        + [pltpu.VMEM(result.shape, f32) for result in out_shape]
        + [
            pltpu.VMEM((n_bus, block, buses), f32),
            pltpu.VMEM((2, buses, LANES), jnp.bfloat16),
            pltpu.VMEM((3, hours, width), f32),
            pltpu.VMEM((3, hours, width), f32),
            pltpu.VMEM((chips, block, LANES), f32),
            pltpu.VMEM((chips, block, LANES), f32),
            pltpu.VMEM((2 * width, chips * block), jnp.bfloat16),
            pltpu.VMEM((chips, block, 2 * width), jnp.bfloat16),
            pltpu.VMEM((chips, hours, block), f32),
            pltpu.VMEM((ITERS, chips, hours, block), f32),
            pltpu.VMEM((ITERS, chips, hours, block), f32),
            pltpu.VMEM((ITERS, chips, hours, block), f32),
            pltpu.VMEM((ITERS, hours, width), f32),
            pltpu.VMEM((ITERS, hours, width), f32),
            dma((len(arrays) - 1,)),
            dma((4,)),
            dma((n_bus,)),
            dma((2,)),
            dma((2, chips)),
            dma((ITERS, PARTS, chips)),
            dma((ITERS, PARTS, chips)),
            dma((ITERS, PARTS, chips)),
            dma((ITERS, PARTS, chips)),
            dma((ITERS, PARTS, 2)),
        ],
        compiler_params=pltpu.CompilerParams(
            collective_id=0, has_side_effects=True, vmem_limit_bytes=VMEM_BYTES
        ),
    )(*arrays)
    gen_new, charge_new, dual_new, energy_new = pl.pallas_call(
        store_kernel,
        out_shape=out_shape,
        in_specs=[hbm] * 4,
        out_specs=(hbm,) * 4,
        scratch_shapes=[pltpu.VMEM(result.shape, f32) for result in out_shape] + [dma((2, 4))],
        compiler_params=pltpu.CompilerParams(vmem_limit_bytes=VMEM_BYTES),
    )(*results)
    return gen_new.T, charge_new, dual_new.T, energy_new


def on_device(
    generation,
    charging,
    flow_dual,
    energy_dual,
    shift_factors,
    load_units,
    generator_bus,
    storage_bus,
    generator_cost,
    generator_max,
    charging_max,
    energy_init,
    energy_max,
    line_max,
):
    bus_local = shift_factors.shape[1]
    gen_local = generator_bus.shape[0]
    stor_local = storage_bus.shape[0]
    own_index = lax.axis_index("bus")
    bus_ids = lax.broadcasted_iota(jnp.int32, (bus_local, 1), 0) + own_index * bus_local
    gen_onehot = (generator_bus[None, :] == bus_ids).astype(jnp.float32)
    stor_onehot = (storage_bus[None, :] == bus_ids).astype(jnp.float32)
    columns = contract(shift_factors, jnp.concatenate([gen_onehot, stor_onehot], axis=1), inner_pair)
    demand = load_units.astype(jnp.float32) * load_unit
    demand_flows = contract(shift_factors, demand, inner_pair)
    unit_cost = generator_cost[:, None]
    ceiling = generator_max[:, None]
    first_slot = own_index * stor_local
    charge_limit = lax.dynamic_slice_in_dim(charging_max, first_slot, stor_local)[None, :]
    start_energy = lax.dynamic_slice_in_dim(energy_init, first_slot, stor_local)[None, :]
    energy_limit = lax.dynamic_slice_in_dim(energy_max, first_slot, stor_local)[None, :]
    for iteration in range(ITERS):
        prices = contract(columns, lax.all_gather(flow_dual, "bus", axis=0, tiled=True), across_first)
        gen_step = jnp.clip(
            generation - primal_step * (unit_cost + prices[:gen_local]), 0.0, ceiling
        )
        gen_bar = 2.0 * gen_step - generation
        stor_prices = prices[gen_local:].T
        gradient = efficiency * interval * reverse_cumsum(energy_dual) - stor_prices
        charge_step = jnp.clip(charging - primal_step * gradient, -charge_limit, charge_limit)
        bar_bus = 2.0 * charge_step - charging
        energy = start_energy + efficiency * interval * jnp.cumsum(bar_bus, axis=0)
        energy_dual = clip_dual(energy_dual + energy_step * energy, energy_step, 0.0, energy_limit)
        charging = charge_step
        bars = jnp.concatenate([gen_bar, -bar_bus.T], axis=0)
        line_flows = lax.psum_scatter(
            contract(columns, bars, inner_pair) - demand_flows, "bus", scatter_dimension=0, tiled=True
        )
        flow_dual = clip_dual(
            flow_dual + dual_step * line_flows, dual_step, -line_max[:, None], line_max[:, None]
        )
        generation = gen_step
    return (generation, charging, flow_dual, energy_dual)


def fits_kernel(n_bus, generation, charging, flow_dual, shift_factors, storage_bus):
    units = generation.shape[0] // n_bus
    stors = storage_bus.shape[0] // n_bus
    block = flow_dual.shape[0] // n_bus
    hours = charging.shape[0] // 2
    buses = shift_factors.shape[1] // n_bus
    return (
        n_bus % 2 == 0
        and units == stors
        and 4 * units == LANES
        and hours == 16
        and block % LANES == 0
        and buses % LANES == 0
        and shift_factors.shape[0] * buses * 4 <= 2**24
    )


def solution(mesh):
    placed = (
        P("bus", "groups"),
        P("groups", "bus"),
        P("bus", "groups"),
        P("groups", "bus"),
        P(None, "bus"),
        P("bus", "groups"),
        P("bus"),
        P("bus"),
        P("bus"),
        P("bus"),
        P(),
        P(),
        P(),
        P("bus"),
    )
    n_bus = mesh.shape["bus"]

    def whole(*arrays):
        fits = mesh.shape["groups"] == 2 and fits_kernel(
            n_bus, arrays[0], arrays[1], arrays[2], arrays[4], arrays[7]
        )
        return jax.shard_map(
            on_device_kernel if fits else on_device,
            mesh=mesh,
            in_specs=placed,
            out_specs=(P("bus", "groups"), P("groups", "bus"), P("bus", "groups"), P("groups", "bus")),
            check_vma=False,
        )(*arrays)

    return whole
```
